32 devices in a mesh: dp: 4 (over y, x), fsdp: 8 (over z, core).
Axes of the slice: x: 2, y: 2, z: 4, core: 2. Of those that a mesh axis runs over, the one named last changes fastest.
Arguments:
- latents: bfloat16 [128, 1024], P(None, ('dp', 'fsdp')), may hold values from -6 to 6
- gain_q: bfloat16 [1024], P(('dp', 'fsdp')), may hold values from 0.5 to 1.5
- gain_kv: bfloat16 [1024], P(('dp', 'fsdp')), may hold values from 0.5 to 1.5
- w_q: bfloat16 [1024, 1024], P(('dp', 'fsdp')), may hold values from -0.1875 to 0.1875
- w_k: bfloat16 [1024, 1024], P(('dp', 'fsdp')), may hold values from -0.1875 to 0.1875
- w_v: bfloat16 [1024, 1024], P(('dp', 'fsdp')), may hold values from -0.1875 to 0.1875
- w_o: bfloat16 [1024, 1024], P(('dp', 'fsdp')), may hold values from -0.75 to 0.75
- gain_s: bfloat16 [1024], P(('dp', 'fsdp')), may hold values from 0.5 to 1.5
- s_q: bfloat16 [1024, 1024], P(('dp', 'fsdp')), may hold values from -0.1875 to 0.1875
- s_k: bfloat16 [1024, 1024], P(('dp', 'fsdp')), may hold values from -0.1875 to 0.1875
- s_v: bfloat16 [1024, 1024], P(('dp', 'fsdp')), may hold values from -0.1875 to 0.1875
- s_o: bfloat16 [1024, 1024], P(('dp', 'fsdp')), may hold values from -0.5 to 0.5
- gain_m: bfloat16 [1024], P(('dp', 'fsdp')), may hold values from 0.5 to 1.5
- w_up: bfloat16 [1024, 4096], P(('dp', 'fsdp')), may hold values from -0.1875 to 0.1875
- w_down: bfloat16 [4096, 1024], P(('dp', 'fsdp')), may hold values from -0.09375 to 0.09375
- points: bfloat16 [65536, 1024], P(('dp', 'fsdp')), may hold values from -6 to 6
- neighbours: int32 [128, 512], P(('dp', 'fsdp')), may hold values from 0 to 2047
- lengths: int32 [128], P(('dp', 'fsdp')), may hold values from 97 to 512, as said below
- cotangent: bfloat16 [16384, 1024], P(('dp', 'fsdp')), may hold values from -6 to 6
Outputs:
- output: bfloat16 [16384, 1024], P(('dp', 'fsdp'))
- point_grad: bfloat16 [65536, 1024], P(('dp', 'fsdp'))
- grad_latents: float32 [128, 1024], P(None, ('dp', 'fsdp'))
- grad_gain_q: float32 [1024], P(('dp', 'fsdp'))
- grad_gain_kv: float32 [1024], P(('dp', 'fsdp'))
- grad_w_q: float32 [1024, 1024], P(('dp', 'fsdp'))
- grad_w_k: float32 [1024, 1024], P(('dp', 'fsdp'))
- grad_w_v: float32 [1024, 1024], P(('dp', 'fsdp'))
- grad_w_o: float32 [1024, 1024], P(('dp', 'fsdp'))
- grad_gain_s: float32 [1024], P(('dp', 'fsdp'))
- grad_s_q: float32 [1024, 1024], P(('dp', 'fsdp'))
- grad_s_k: float32 [1024, 1024], P(('dp', 'fsdp'))
- grad_s_v: float32 [1024, 1024], P(('dp', 'fsdp'))
- grad_s_o: float32 [1024, 1024], P(('dp', 'fsdp'))
- grad_gain_m: float32 [1024], P(('dp', 'fsdp'))
- grad_w_up: float32 [1024, 4096], P(('dp', 'fsdp'))
- grad_w_down: float32 [4096, 1024], P(('dp', 'fsdp'))
The draws below stay inside these ranges and needn't reach their ends.
Inputs may be any that keep to these rules, and one draw needn't show every extreme that they name: Group g reads point (g // 4) * 2048 + neighbours[g, j] of its own block. The first lengths[g] neighbour slots of group g are live; some group has all 512.
All inputs are finite; a program needn't handle non-finite values.
Results may differ from the reference program's by a relative error of at most 0.019.
Values may be sent and summed in bfloat16 or wider, within the bound.
A program may use at most 256 MiB of HBM per device.

```python
import jax
import jax.numpy as jnp
from jax import lax

HEADS = 8
HEAD = 128
D = 1024
FF = 4096
LAT = 128
NEIGH = 512
G_DEV = 4
P_DEV = 2048
GROUPS = 128
ROWS = 16384
POINTS = 65536


def draw_lengths(key, part):
    key = jax.random.fold_in(key, 7)
    key_shift, key_cut, key_full = jax.random.split(key, 3)
    shifts = jax.random.randint(key_shift, (GROUPS,), 0, 3)
    top_counts = jnp.right_shift(jnp.full((GROUPS,), NEIGH, jnp.int32), shifts)
    cut_counts = jax.random.randint(key_cut, (GROUPS,), 0, jnp.maximum(top_counts // 4, 1))
    counts = top_counts - cut_counts
    least_count = NEIGH // 4 - max(NEIGH // 16, 1) + 1
    full_at = jax.random.randint(key_full, (), 0, GROUPS)
    least_at = (full_at + 1) % GROUPS
    counts = counts.at[least_at].set(least_count)
    return counts.at[full_at].set(NEIGH).astype(jnp.int32)


def plant(drawn, key, smallest, high):
    longest = drawn.shape.index(max(drawn.shape))
    spots = []
    for shift in (0, 1):
        where = [jax.random.randint(jax.random.fold_in(key, axis), (), 0, length) for axis, length in enumerate(drawn.shape)]
        where[longest] = (where[longest] + shift) % drawn.shape[longest]
        spots.append(tuple(where))
    return drawn.at[spots[0]].set(smallest).at[spots[1]].set(high)


def raised(drawn, rng, source, target, blocks, factor):
    def block_of(position):
        return (jnp.arange(drawn.shape[position]) // (drawn.shape[position] // blocks)).reshape((-1,) + (1,) * (drawn.ndim - 1 - position))

    first = jax.random.permutation(rng, blocks)[block_of(target)]
    other_side = (block_of(target) + blocks // 2) % blocks
    return jnp.where((block_of(source) == first) | (block_of(source) == other_side), factor * drawn, drawn)


def shard_levels(own_key, dims, shards, smallest, high):
    def one(axis_at, parts):
        draws = jax.random.uniform(jax.random.fold_in(jax.random.fold_in(own_key, 6), axis_at), (parts,), jnp.float32, smallest / len(shards), high / len(shards))
        return jnp.repeat(jnp.exp(draws), dims[axis_at] // parts).reshape((-1,) + (1,) * (len(dims) - axis_at - 1))

    gain = one(*shards[0])
    for cut in shards[1:]:
        gain = gain * one(*cut)
    return gain


def bell_draw(key, shape, scale, limit, cuts=(), kind=jnp.bfloat16):
    drawn = scale * jax.random.normal(key, shape, jnp.float32)
    if cuts:
        drawn = drawn * shard_levels(key, shape, cuts, -0.22, 0.18)
    return jnp.clip(drawn, -limit, limit).astype(kind)


def noise_with(rng, extent, scale, reach, shards, heavy, kind=jnp.bfloat16):
    entries = scale * jax.random.normal(rng, extent, jnp.float32)
    if shards:
        entries = entries * shard_levels(rng, extent, shards, -0.22, 0.18)
    return jnp.clip(raised(entries, jax.random.fold_in(rng, 3), *heavy), -reach, reach).astype(kind)


def setup_inputs(seed: int = 0) -> dict:
    streams_of = jax.random.split(jax.random.key(seed), 20)
    return {
        "latents": bell_draw(streams_of[0], (LAT, D), 1.0, 6.0, ((1, 32),)),
        "gain_q": jnp.clip(1.0 + 0.1 * jax.random.normal(streams_of[1], (D,), jnp.float32), 0.5, 1.5).astype(jnp.bfloat16),
        "gain_kv": jnp.clip(1.0 + 0.1 * jax.random.normal(streams_of[2], (D,), jnp.float32), 0.5, 1.5).astype(jnp.bfloat16),
        "w_q": bell_draw(streams_of[3], (D, D), D ** -0.5, 0.1875, ((0, 32),)),
        "w_k": bell_draw(streams_of[4], (D, D), D ** -0.5, 0.1875, ((0, 32),)),
        "w_v": bell_draw(streams_of[5], (D, D), D ** -0.5, 0.1875, ((0, 32),)),
        "w_o": bell_draw(streams_of[6], (D, D), (D // 16) ** -0.5, 0.75, ((0, 32),)),
        "gain_s": jnp.clip(1.0 + 0.1 * jax.random.normal(streams_of[7], (D,), jnp.float32), 0.5, 1.5).astype(jnp.bfloat16),
        "s_q": bell_draw(streams_of[8], (D, D), D ** -0.5, 0.1875, ((0, 32),)),
        "s_k": bell_draw(streams_of[9], (D, D), D ** -0.5, 0.1875, ((0, 32),)),
        "s_v": bell_draw(streams_of[10], (D, D), D ** -0.5, 0.1875, ((0, 32),)),
        "s_o": bell_draw(streams_of[11], (D, D), (D // 8) ** -0.5, 0.5, ((0, 32),)),
        "gain_m": jnp.clip(1.0 + 0.1 * jax.random.normal(streams_of[12], (D,), jnp.float32), 0.5, 1.5).astype(jnp.bfloat16),
        "w_up": bell_draw(streams_of[13], (D, FF), D ** -0.5, 0.1875, ((0, 32),)),
        "w_down": bell_draw(streams_of[14], (FF, D), FF ** -0.5, 0.09375, ((0, 32),)),
        "points": bell_draw(streams_of[15], (POINTS, D), 1.0, 6.0, ((0, 32),)),
        "neighbours": plant(jax.random.randint(streams_of[16], (GROUPS, NEIGH), 0, P_DEV), jax.random.fold_in(streams_of[16], 1), 0, P_DEV - 1).astype(jnp.int32),
        "lengths": draw_lengths(jax.random.fold_in(streams_of[19], 71), 0),
        "cotangent": noise_with(streams_of[18], (ROWS, D), 1.0, 6.0, ((0, 32),), (0, 1, 32, 2.75)),
    }


@jax.custom_vjp
def low(v):
    return lax.optimization_barrier(v.astype(jnp.bfloat16)).astype(jnp.float32)

@jax.custom_vjp
def low_back(v):
    return v

def low_keep(v):
    return (low(v), None)

def low_pass(kept, grad):
    return (grad,)

def back_keep(v):
    return (v, None)

def back_low(kept, grad):
    return (low(grad),)
low.defvjp(low_keep, low_pass)
low_back.defvjp(back_keep, back_low)
EPSILON = 1e-05
MASK_FILL = -1e+30
HIGHEST_PREC = lax.Precision.HIGHEST

def layer_norm(row_data, gain_vec):
    row_mean = lax.optimization_barrier(jnp.mean(row_data, axis=-1, keepdims=True))
    centred = row_data - row_mean
    spread = lax.optimization_barrier(jnp.mean(centred * centred, axis=-1, keepdims=True))
    return centred * lax.rsqrt(spread + EPSILON) * gain_vec

def gelu_tanh(values):
    inner = 0.7978845608028654 * (values + 0.044715 * values * values * values)
    return 0.5 * values * (1.0 + jnp.tanh(inner))

def matmul(left_op, right_op):
    return jnp.dot(left_op, right_op, precision=HIGHEST_PREC)

def softmax_rows(scores):
    top_score = lax.optimization_barrier(jnp.max(scores, axis=-1, keepdims=True))
    exp_terms = jnp.exp(scores - top_score)
    return exp_terms / lax.optimization_barrier(jnp.sum(exp_terms, axis=-1, keepdims=True))

def block_forward(params, point_rows, neigh_rows, length_rows):
    latents, gain_q, gain_kv, w_q, w_k, w_v, w_o, gain_s, s_q, s_k, s_v, s_o, gain_m, w_up, w_down = params
    groups = neigh_rows.shape[0]
    score_scale = HEAD ** (-0.5)
    h_q = low(layer_norm(latents, gain_q))
    query = low(low_back(matmul(h_q, w_q)))
    h_p = low(layer_norm(point_rows, gain_kv))
    key_pts = low(low_back(matmul(h_p, w_k)))
    value_pts = low(low_back(matmul(h_p, w_v)))
    flat_index = neigh_rows.reshape(-1)
    keys_g = jnp.take(key_pts, flat_index, axis=0).reshape(groups, NEIGH, HEADS, HEAD)
    values_g = jnp.take(value_pts, flat_index, axis=0).reshape(groups, NEIGH, HEADS, HEAD)
    query_h = query.reshape(LAT, HEADS, HEAD)
    raw_scores = jnp.einsum('qhe,gkhe->ghqk', query_h, keys_g, precision=HIGHEST_PREC) * score_scale
    scores = low_back(raw_scores)
    live_mask = (jnp.arange(NEIGH, dtype=jnp.int32)[None, :] < length_rows[:, None])[:, None, None, :]
    scores = jnp.where(live_mask, scores, MASK_FILL)
    cross_probs = low(softmax_rows(scores))
    cross_mix = low(low_back(jnp.einsum('ghqk,gkhe->gqhe', cross_probs, values_g, precision=HIGHEST_PREC)))
    cross_out = low_back(matmul(cross_mix.reshape(groups * LAT, D), w_o))
    resid_one = (latents[None] + cross_out.reshape(groups, LAT, D)).reshape(groups * LAT, D)
    h_s = low(layer_norm(resid_one, gain_s))
    self_q = low(low_back(matmul(h_s, s_q))).reshape(groups, LAT, HEADS, HEAD)
    self_k = low(low_back(matmul(h_s, s_k))).reshape(groups, LAT, HEADS, HEAD)
    self_v = low(low_back(matmul(h_s, s_v))).reshape(groups, LAT, HEADS, HEAD)
    self_scores = low_back(jnp.einsum('gqhe,gkhe->ghqk', self_q, self_k, precision=HIGHEST_PREC) * score_scale)
    self_probs = low(softmax_rows(self_scores))
    self_mix = low(low_back(jnp.einsum('ghqk,gkhe->gqhe', self_probs, self_v, precision=HIGHEST_PREC)))
    resid_two = resid_one + low_back(matmul(self_mix.reshape(groups * LAT, D), s_o))
    h_m = low(layer_norm(resid_two, gain_m))
    up_vals = low_back(matmul(h_m, w_up))
    act_vals = low(gelu_tanh(up_vals))
    return resid_two + low_back(matmul(act_vals, w_down))

def reference(latents, gain_q, gain_kv, w_q, w_k, w_v, w_o, gain_s, s_q, s_k, s_v, s_o, gain_m, w_up, w_down, points, neighbours, lengths, cotangent):
    params = tuple((weight_arr.astype(jnp.float32) for weight_arr in (latents, gain_q, gain_kv, w_q, w_k, w_v, w_o, gain_s, s_q, s_k, s_v, s_o, gain_m, w_up, w_down)))
    block_count = GROUPS // G_DEV
    point_blocks = points.astype(jnp.float32).reshape(block_count, P_DEV, D)
    neigh_blocks = neighbours.astype(jnp.int32).reshape(block_count, G_DEV, NEIGH)
    length_blocks = lengths.astype(jnp.int32).reshape(block_count, G_DEV)

    def forward(param_set, point_set):

        def one_block(block_args):
            return block_forward(param_set, block_args[0], block_args[1], block_args[2])
        return lax.map(jax.checkpoint(one_block), (point_set, neigh_blocks, length_blocks))
    result, pullback = jax.vjp(forward, params, point_blocks)
    grads, point_grad = pullback(cotangent.astype(jnp.float32).reshape(block_count, G_DEV * LAT, D))
    return (result.reshape(ROWS, D).astype(jnp.bfloat16), point_grad.reshape(POINTS, D).astype(jnp.bfloat16), grads[0], grads[1], grads[2], grads[3], grads[4], grads[5], grads[6], grads[7], grads[8], grads[9], grads[10], grads[11], grads[12], grads[13], grads[14])
```

```python
import functools

import jax
import jax.numpy as jnp
from jax import lax
from jax.experimental import pallas as pl
from jax.experimental.pallas import tpu as pltpu
from jax.sharding import PartitionSpec as P

HEADS = 8
HEAD = 128
D = 1024
FF = 4096
LAT = 128
NEIGH = 512

EPSILON = 1e-05
MASK_FILL = -1e30
SCALE = HEAD**-0.5
GELU_K = 0.7978845608028654
GELU_C = 0.044715

AXES = ("dp", "fsdp")
MESH = pl.DeviceIdType.MESH
F32 = jnp.float32
BF16 = jnp.bfloat16

LINKED_MESH = (4, 8)
PARTS = 32
PART = D // PARTS
SMALL = 256
QUARTERS = FF // D

W_K, W_V, W_Q, W_O, S_Q, S_K, S_V, S_O, UP, DOWN = 0, 1, 2, 3, 4, 5, 6, 7, 8, 12
CHUNKS = 16
TINY = CHUNKS

Y, X, ZH, ZL, CORE = range(5)
STAGES = 5
GATHER_ORDERS = ((ZL, ZH, X, Y, CORE), (ZL, ZH, Y, X, CORE), (ZH, X, Y, ZL, CORE), (ZH, Y, X, ZL, CORE))
GATHER_MIX = (0, 1, 0, 1, 2, 3)
GATHER_LAG = 4
REDUCE_ORDERS = tuple(tuple(reversed(order)) for order in GATHER_ORDERS)
LAND_SLOTS = 3
TERM_SLOTS = 2
WEIGHT_SLOTS = 3
LOADS = tuple(range(CHUNKS)) + tuple(range(UP, DOWN)) + (S_O, S_Q, S_K, S_V, W_O, W_Q, W_K, W_V)
QUEUE = tuple(range(DOWN, CHUNKS)) + tuple(range(UP, DOWN)) + (S_O, S_Q, S_K, S_V, W_O, W_K, W_V, W_Q, TINY)


def dot_nn(left, right):
    return jnp.dot(left, right, preferred_element_type=F32)


def dot_nt(left, right):
    return lax.dot_general(left, right, (((1,), (1,)), ((), ())), preferred_element_type=F32)


def dot_tn(left, right):
    return lax.dot_general(left, right, (((0,), (0,)), ((), ())), preferred_element_type=F32)


def row_mean(rows):
    return jnp.mean(rows, axis=-1, keepdims=True)


def normalised(rows):
    centred = rows - row_mean(rows)
    inv = lax.rsqrt(row_mean(centred * centred) + EPSILON)
    return centred * inv, inv


def norm_back(rows, gain, grad):
    unit, inv = normalised(rows)
    scaled = grad * gain
    pull = inv * (scaled - row_mean(scaled) - unit * row_mean(scaled * unit))
    return pull, jnp.sum(grad * unit, axis=0, keepdims=True), unit


def bits_of():
    row, col = lax.axis_index("dp"), lax.axis_index("fsdp")
    return (row // 2, row % 2, col // 4, (col // 2) % 2, col % 2)


def across(bits, axis):
    other = [1 - bit if at == axis else bit for at, bit in enumerate(bits)]
    return (other[Y] * 2 + other[X], other[ZH] * 4 + other[ZL] * 2 + other[CORE])


class Gather:
    def __init__(self, refs, bits):
        self.refs, self.bits = refs, bits
        self.pieces = [(TINY, 0, PART, GATHER_ORDERS[0])]
        for chunk in range(CHUNKS):
            for half in range(2):
                order = GATHER_ORDERS[GATHER_MIX[(2 * chunk + half) % len(GATHER_MIX)]]
                self.pieces.append((chunk, half * (PART // 2), PART // 2, order))
        self.ticks = len(self.pieces) + STAGES * GATHER_LAG
        self.now, self.done, self.own = 0, 0, False

    def shard(self, chunk, row, rows):
        if chunk == TINY:
            return self.refs["small"].at[pl.ds(row, rows)]
        if chunk < UP:
            return self.refs["attn"][chunk].at[pl.ds(row, rows)]
        if chunk < DOWN:
            return self.refs["up"].at[chunk - UP, pl.ds(row, rows)]
        return self.refs["down"].at[pl.ds((chunk - DOWN) * PART + row, rows)]

    def place(self, chunk, index, row, rows):
        if chunk == TINY:
            return self.refs["full_small"].at[(*index, pl.ds(row, rows))]
        return self.refs["full"].at[(chunk, *index, pl.ds(row, rows))]

    def own_copies(self):
        for chunk in range(CHUNKS + 1):
            yield pltpu.make_async_copy(
                self.shard(chunk, 0, PART), self.place(chunk, self.bits, 0, PART), self.refs["own_sem"].at[chunk]
            )

    def copy(self, piece, stage):
        chunk, row, rows, order = self.pieces[piece]
        if stage == 0:
            source, target = self.shard(chunk, row, rows), self.place(chunk, self.bits, row, rows)
        else:
            index = [pl.ds(0, 2) if axis in order[:stage] else self.bits[axis] for axis in range(5)]
            source = target = self.place(chunk, index, row, rows)
        return pltpu.make_async_remote_copy(
            src_ref=source,
            dst_ref=target,
            send_sem=self.refs["g_send"].at[piece, stage],
            recv_sem=self.refs["g_recv"].at[piece, stage],
            device_id=across(self.bits, order[stage]),
            device_id_type=MESH,
        )

    def start(self):
        for copy in self.own_copies():
            copy.start()

    def tick(self):
        if self.now >= self.ticks:
            return
        for stage in range(STAGES, -1, -1):
            piece = self.now - stage * GATHER_LAG
            if not 0 <= piece < len(self.pieces):
                continue
            if stage > 0:
                if not self.own:
                    self.own = True
                    for copy in self.own_copies():
                        copy.wait()
                self.copy(piece, stage - 1).wait_recv()
            if stage < STAGES:
                self.copy(piece, stage).start()
            else:
                self.done = piece + 1
        self.now += 1

    def need(self, chunk):
        last = 0 if chunk == TINY else 2 * chunk + 2
        while self.done <= last:
            self.tick()

    def finish(self):
        while self.now < self.ticks:
            self.tick()
        for piece in range(len(self.pieces)):
            for stage in range(STAGES):
                self.copy(piece, stage).wait_send()


class Reduce:
    def __init__(self, refs, bits):
        self.refs, self.bits = refs, bits
        self.lands = [refs[f"land{stage}"] for stage in range(STAGES)]
        self.now, self.begun = 0, []

    def pieces(self, at):
        if QUEUE[at] == TINY:
            return [(0, 0, SMALL, REDUCE_ORDERS[0])]
        return [(0, 0, 384, REDUCE_ORDERS[0]), (1, 384, 384, REDUCE_ORDERS[1]), (2, 768, 256, REDUCE_ORDERS[2 + at % 2])]

    def open_axes(self, order, stage):
        return [axis for axis in range(5) if axis not in order[: stage + 1]]

    def kept(self, order, stage, spot):
        return [self.bits[one] if one == order[stage] else spot(one) for one in self.open_axes(order, stage - 1)]

    def copy(self, at, stage, piece):
        number, col, cols, order = piece
        slot, span = at % LAND_SLOTS, pl.ds(col, cols)
        every = pl.ds(0, 2)
        if stage == 0:
            source = self.refs["term"].at[(at % TERM_SLOTS, 1 - self.bits[CORE], *[every] * 4, pl.ds(0, PART), span)]
        else:
            index = [
                1 - self.bits[one] if one == order[stage] else every for one in self.open_axes(order, stage - 1)
            ]
            source = self.lands[stage - 1].at[(slot, *index, pl.ds(0, PART), span)]
        target = self.lands[stage].at[(slot, *[every] * (4 - stage), pl.ds(0, PART), span)]
        return pltpu.make_async_remote_copy(
            src_ref=source,
            dst_ref=target,
            send_sem=self.refs["r_send"].at[at, stage, number],
            recv_sem=self.refs["r_recv"].at[at, stage, number],
            device_id=across(self.bits, order[stage]),
            device_id_type=MESH,
        )

    def credit(self, stage, number, axis):
        return self.refs["credit"].at[stage, number, axis]

    def release(self, at, stage):
        later = at + LAND_SLOTS
        if later >= len(QUEUE):
            return
        for number, _, _, order in self.pieces(later):
            axis = order[stage]
            pl.semaphore_signal(
                self.credit(stage, number, axis), inc=1, device_id=across(self.bits, axis), device_id_type=MESH
            )

    def send(self, at, stage):
        for piece in self.pieces(at):
            if at >= LAND_SLOTS:
                pl.semaphore_wait(self.credit(stage, piece[0], piece[3][stage]), 1)
            self.copy(at, stage, piece).start()

    def add(self, at, stage, piece):
        number, col, cols, order = piece
        slot, span, land = at % LAND_SLOTS, pl.ds(col, cols), self.lands[stage]
        left = self.open_axes(order, stage)

        def step(i, carry):
            index = [(i >> (len(left) - 1 - k)) & 1 for k in range(len(left))]
            if stage == 0:
                extra = self.refs["term"][(at % TERM_SLOTS, self.bits[CORE], *index, slice(None), span)]
            else:
                kept = self.kept(order, stage, dict(zip(left, index)).get)
                extra = self.lands[stage - 1][(slot, *kept, slice(None), span)]
            land[(slot, *index, slice(None), span)] += extra
            return carry

        lax.fori_loop(0, 1 << len(left), step, 0)

    def advance(self, at, stage):
        pieces = self.pieces(at)
        last = stage == STAGES
        slot = at % LAND_SLOTS
        if last:
            self.final_ready(at)
        for piece in pieces:
            self.copy(at, stage - 1, piece).wait_recv()
        if stage == 1:
            self.add(at, 0, (0, 0, SMALL if QUEUE[at] == TINY else D, pieces[0][3]))
        else:
            for piece in pieces:
                if last:
                    _, col, cols, order = piece
                    span = pl.ds(col, cols)
                    mine = self.lands[3][(slot, *self.kept(order, 4, None), slice(None), span)]
                    came = self.lands[4][slot, :, span]
                    self.refs["final"][at % 2, :, span] = mine.astype(F32) + came.astype(F32)
                else:
                    self.add(at, stage - 1, piece)
        if last:
            self.final_copy(at).start()
        else:
            self.send(at, stage)
        for piece in pieces:
            self.copy(at, stage - 1, piece).wait_send()
        if stage >= 2:
            self.release(at, stage - 2)
        if last:
            self.release(at, 4)

    def final_copy(self, at):
        chunk = QUEUE[at]
        source, sem = self.refs["final"].at[at % 2], self.refs["final_sem"].at[at % 2]
        if chunk == TINY:
            source, target = source.at[:, pl.ds(0, SMALL)], self.refs["g_small"]
        elif chunk < UP:
            target = self.refs["g_attn"][chunk]
        elif chunk < DOWN:
            target = self.refs["g_up"].at[chunk - UP]
        else:
            target = self.refs["g_down"].at[pl.ds((chunk - DOWN) * PART, PART)]
        return pltpu.make_async_copy(source, target, sem)

    def final_ready(self, at):
        if at >= 2:
            self.final_copy(at - 2).wait()

    def tick(self, tile):
        for at, began in enumerate(self.begun):
            if 1 <= self.now - began <= STAGES:
                self.advance(at, self.now - began)
        if tile is not None and len(self.begun) < len(QUEUE):
            at = len(self.begun)
            width = SMALL if QUEUE[at] == TINY else D
            for i in range(2):
                value = tile(QUEUE[at], i).astype(BF16).reshape(8, 2, PART, width)
                for core in range(2):
                    for j in range(8):
                        index = (at % TERM_SLOTS, core, i, j >> 2, (j >> 1) & 1, j & 1, slice(None), pl.ds(0, width))
                        self.refs["term"][index] = value[j, core]
            self.send(at, 0)
            self.begun.append(self.now)
        self.now += 1

    def finish(self):
        assert len(self.begun) == len(QUEUE)
        while self.now - self.begun[-1] <= STAGES:
            self.tick(None)
        for at in (len(QUEUE) - 2, len(QUEUE) - 1):
            self.final_copy(at).wait()


class Local:
    def __init__(self, refs):
        self.refs, self.count, self.tiles = refs, 0, 0

    def copy(self, tile):
        chunk, half = QUEUE[tile // 2], tile % 2
        rows = pl.ds(half * 512, 512)
        if chunk < UP:
            target = self.refs["g_attn"][chunk].at[rows]
        elif chunk < DOWN:
            target = self.refs["g_up"].at[chunk - UP, rows]
        else:
            target = self.refs["g_down"].at[pl.ds((chunk - DOWN) * D + half * 512, 512)]
        return pltpu.make_async_copy(self.refs["term"].at[half], target, self.refs["term_sem"].at[half])

    def tick(self, tile):
        if tile is None or self.count >= len(QUEUE):
            return
        chunk = QUEUE[self.count]
        self.count += 1
        for half in range(2):
            value = tile(chunk, half)
            if chunk == TINY:
                self.refs["g_small"][pl.ds(half * 512, 512), :] = value
                continue
            if self.tiles >= 2:
                self.copy(self.tiles - 2).wait()
            self.refs["term"][half] = value.astype(BF16)
            self.copy(self.tiles).start()
            self.tiles += 1

    def finish(self):
        assert self.count == len(QUEUE)
        for tile in (self.tiles - 2, self.tiles - 1):
            self.copy(tile).wait()


class Weights:
    def __init__(self, refs, gather):
        self.refs, self.gather = refs, gather
        self.fetched, self.used = 0, 0

    def copy(self, at):
        chunk = LOADS[at]
        if self.gather is not None:
            source = self.refs["full"].at[chunk]
        elif chunk < UP:
            source = self.refs["attn"][chunk]
        elif chunk < DOWN:
            source = self.refs["up"].at[chunk - UP]
        else:
            source = self.refs["down"].at[chunk - DOWN]
        slot = at % WEIGHT_SLOTS
        return pltpu.make_async_copy(source, self.refs["held"].at[slot], self.refs["held_sem"].at[slot])

    def fetch(self, limit):
        while self.fetched < min(limit, len(LOADS)):
            if self.gather is not None:
                self.gather.need(LOADS[self.fetched])
            self.copy(self.fetched).start()
            self.fetched += 1

    def use(self, chunk, keep=0):
        at = self.used
        assert LOADS[at] == chunk
        self.fetch(at + 1)
        if at >= CHUNKS:
            self.fetch(at + WEIGHT_SLOTS - keep)
        self.copy(at).wait()
        self.used += 1
        return lambda: self.refs["held"][at % WEIGHT_SLOTS].reshape(D, D)


NAMES_IN = ("small", "w_k", "w_v", "w_q", "w_o", "s_q", "s_k", "s_v", "s_o", "up", "down", "points", "near", "lens", "cot")
NAMES_OUT = ("out", "point_grad", "g_small", "g_k", "g_v", "g_q", "g_o", "gs_q", "gs_k", "gs_v", "gs_o", "g_up", "g_down")


def layer_kernel(linked, names, *refs):
    r = dict(zip(names, refs, strict=True))
    r["attn"] = [r[name] for name in NAMES_IN[1:9]]
    r["g_attn"] = [r[name] for name in NAMES_OUT[3:11]]
    points, near, lens, cot = r["points"], r["near"], r["lens"], r["cot"]
    keys, values, wide, slope = r["keys"], r["values"], r["wide"], r["slope"]
    cross_mix, self_mix, h_s, h_m = r["cross_mix"], r["self_mix"], r["h_s"], r["h_m"]
    self_q, self_k, self_v = r["self_q"], r["self_k"], r["self_v"]
    two_low, one_low, mix_grad = r["two_low"], r["one_low"], r["mix_grad"]
    res_one, res_two, grad, part = r["res_one"], r["res_two"], r["grad"], r["part"]
    scores, score_grad, lat, lat_grad = r["scores"], r["score_grad"], r["lat"], r["lat_grad"]
    h_q, query, lse, gains, gain_grads = r["h_q"], r["query"], r["lse"], r["gains"], r["gain_grads"]
    count_log = r["count_log"]
    groups = near.shape[0]
    rows, slots = cot.shape[0], keys.shape[0]
    half = slots // 2

    if linked:
        bits = bits_of()
        barrier = pltpu.get_barrier_semaphore()
        for axis in range(5):
            pl.semaphore_signal(barrier, inc=1, device_id=across(bits, axis), device_id_type=MESH)
        pl.semaphore_wait(barrier, 5)
        gather, reduce = Gather(r, bits), Reduce(r, bits)
        gather.start()
        move = gather.tick
    else:
        gather, reduce = None, Local(r)
        move = lambda: None
    weights = Weights(r, gather)

    point_load = pltpu.make_async_copy(points, slope, r["point_sem"].at[0])
    point_load.start()
    for _ in range(8):
        move()

    for g in range(groups):
        listed = near[pl.ds(g, 1), :]
        live = lax.broadcasted_iota(jnp.int32, (1, NEIGH), 1) < lens[g]
        high = lax.broadcasted_iota(jnp.int32, (slots // 128, NEIGH), 0) == listed // 128
        low = lax.broadcasted_iota(jnp.int32, (128, NEIGH), 0) == listed % 128
        high = jnp.where(high & live, 1.0, 0.0).astype(BF16)
        low = jnp.where(low, 1.0, 0.0).astype(BF16)
        count = dot_nt(high, low)
        count = jnp.where(count > 0.5, jnp.log(jnp.maximum(count, 1.0)), MASK_FILL)
        for a in range(slots // 128):
            count_log[pl.ds(g, 1), pl.ds(a * 128, 128)] = count[a : a + 1, :]

    if linked:
        gather.need(TINY)
        small_load = pltpu.make_async_copy(r["full_small"], r["small_in"], r["tiny_sem"].at[0])
    else:
        small_load = pltpu.make_async_copy(r["small"], r["small_in"], r["tiny_sem"].at[0])
    small_load.start()
    small_load.wait()
    turned = r["small_in"][...].reshape(D, SMALL).astype(F32).T
    lat[...] = turned[:LAT]
    gains[...] = turned[LAT : LAT + 8]
    gain_grads[...] = jnp.zeros_like(gain_grads)
    gain_of = lambda i: gains[pl.ds(i, 1), :]
    h_q[...] = (normalised(lat[...])[0] * gain_of(0)).astype(BF16)
    point_load.wait()

    tile = 64

    def span_of(i, size=tile):
        return pl.ds(pl.multiple_of(i * size, size), size)

    def head_of(h):
        return pl.ds(pl.multiple_of(h * HEAD, HEAD), HEAD)

    def each(count, step):
        def body(i, carry):
            step(i)
            return carry

        lax.fori_loop(0, count, body, 0)

    def norm_points(i):
        at = span_of(i)
        wide[at, :] = (normalised(slope[at, :].astype(F32))[0] * gain_of(1)).astype(BF16)

    each(slots // tile, norm_points)

    for chunk, target in ((W_K, keys), (W_V, values)):
        w = weights.use(chunk)

        def project(i, target=target, w=w):
            at = span_of(i, 512)
            target[at, :] = dot_nn(wide[at, :], w()).astype(BF16)

        each(slots // 512, project)
        move()
    w = weights.use(W_Q)
    query[...] = dot_nn(h_q[...], w()).astype(BF16)

    lane = lax.broadcasted_iota(jnp.int32, (LAT, HEAD), 1)

    def weigh(h):
        hs = head_of(h)
        scores[...] = dot_nt(query[:, hs], keys[:, hs]) * SCALE
        for g in range(groups):
            def softmax(i, g=g):
                at = span_of(i, 32)
                logit = scores[at, :] + count_log[pl.ds(g, 1), :]
                top = jnp.max(logit, axis=-1, keepdims=True)
                terms = jnp.exp(logit - top)
                total = jnp.sum(terms, axis=-1, keepdims=True)
                probs = (terms / total).astype(BF16)
                row = pl.ds(pl.multiple_of(g * LAT + i * 32, 32), 32)
                wide[row, :] = probs[:, :half]
                wide[pl.ds(pl.multiple_of(rows + g * LAT + i * 32, 32), 32), :] = probs[:, half:]
                here = lax.broadcasted_iota(jnp.int32, (32, HEAD), 1) == h
                lse[row, :] = jnp.where(here, top + jnp.log(total), lse[row, :])

            each(LAT // 32, softmax)
        mixed = dot_nn(wide[pl.ds(0, rows), :], values[pl.ds(0, half), hs])
        mixed += dot_nn(wide[pl.ds(rows, rows), :], values[pl.ds(half, half), hs])
        cross_mix[:, hs] = mixed.astype(BF16)

    lse[...] = jnp.zeros_like(lse)
    for part_at in range(4):
        each(2, lambda i, part_at=part_at: weigh(part_at * 2 + i))
        move()
        move()

    w = weights.use(W_O)
    res_one[...] = dot_nn(cross_mix[...], w())

    def add_latents(i):
        at = span_of(i)
        total = res_one[at, :] + lat[span_of(i % (LAT // tile)), :]
        res_one[at, :] = total
        h_s[at, :] = (normalised(total)[0] * gain_of(2)).astype(BF16)

    each(rows // tile, add_latents)
    for chunk, target in ((S_Q, self_q), (S_K, self_k), (S_V, self_v)):
        w = weights.use(chunk)
        target[...] = dot_nn(h_s[...], w()).astype(BF16)

    def group_of(g):
        return pl.ds(g * LAT, LAT)

    def self_probs(g, hs):
        logit = dot_nt(self_q[group_of(g), hs], self_k[group_of(g), hs]) * SCALE
        terms = jnp.exp(logit - jnp.max(logit, axis=-1, keepdims=True))
        return terms / jnp.sum(terms, axis=-1, keepdims=True)

    def self_attend(h):
        hs = head_of(h)
        for g in range(groups):
            probs = self_probs(g, hs).astype(BF16)
            self_mix[group_of(g), hs] = dot_nn(probs, self_v[group_of(g), hs]).astype(BF16)

    each(HEADS, self_attend)
    w = weights.use(S_O)
    res_two[...] = dot_nn(self_mix[...], w())

    def add_first(i):
        at = span_of(i)
        total = res_two[at, :] + res_one[at, :]
        res_two[at, :] = total
        h_m[at, :] = (normalised(total)[0] * gain_of(3)).astype(BF16)

    each(rows // tile, add_first)

    for q in range(QUARTERS):
        w = weights.use(UP + q)

        def expand(i, q=q, w=w):
            u = dot_nn(h_m[span_of(i, 256), :], w())
            square = u * u
            bent = jnp.tanh(GELU_K * (u + GELU_C * square * u))
            at = pl.ds(pl.multiple_of(q * rows + i * 256, 256), 256)
            wide[at, :] = (0.5 * u * (1.0 + bent)).astype(BF16)
            rise = GELU_K * (1.0 + 3.0 * GELU_C * square)
            slope[at, :] = (0.5 * (1.0 + bent) + 0.5 * u * (1.0 - bent * bent) * rise).astype(BF16)

        each(rows // 256, expand)

    def quarter(q):
        return pl.ds(q * rows, rows)

    def terms_of(chunk, i):
        cols = pl.ds(i * 512, 512)
        if chunk == TINY:
            tall = jnp.concatenate((lat_grad[...], gain_grads[...], jnp.zeros((SMALL - LAT - 8, D), F32)), axis=0)
            return tall[:, i * 512 : (i + 1) * 512].T
        if chunk >= DOWN:
            q = chunk - DOWN
            return dot_tn(wide[quarter(q), cols], cot[...])
        if chunk >= UP:
            return dot_tn(h_m[:, cols], slope[quarter(chunk - UP), :])
        left, right = {
            S_O: (self_mix, two_low),
            S_Q: (h_s, self_q),
            S_K: (h_s, self_k),
            S_V: (h_s, self_v),
            W_O: (cross_mix, one_low),
            W_K: (wide, keys),
            W_V: (wide, values),
            W_Q: (h_q, query),
        }[chunk]
        return dot_tn(left[:, cols], right[...])

    def turn(fresh=True):
        reduce.tick(terms_of if fresh else None)

    for q in range(QUARTERS):
        w = weights.use(DOWN + q)
        made = dot_nn(wide[quarter(q), :], w())
        part[...] = made + (res_two[...] if q == 0 else part[...])
        act_grad = dot_nt(cot[...], w())
        slope[quarter(q), :] = (slope[quarter(q), :].astype(F32) * act_grad).astype(BF16)
        turn()
    r["out"][...] = part[...].astype(BF16)
    if linked:
        gather.finish()

    for q in range(QUARTERS):
        w = weights.use(UP + q)
        made = dot_nt(slope[quarter(q), :], w())
        grad[...] = made if q == 0 else grad[...] + made
        if q % 2 == 1:
            turn()

    def gain_add(i, value):
        gain_grads[pl.ds(i, 1), :] += value

    def back_two(i):
        at = span_of(i)
        pull, gain_part, _ = norm_back(res_two[at, :], gain_of(3), grad[at, :])
        total = cot[at, :].astype(F32) + pull
        grad[at, :] = total
        two_low[at, :] = total.astype(BF16)
        gain_add(3, gain_part)

    each(rows // tile, back_two)
    turn()
    w = weights.use(S_O)
    mix_grad[...] = dot_nt(two_low[...], w()).astype(BF16)

    def self_back(h):
        hs = head_of(h)
        for g in range(groups):
            at = group_of(g)
            probs = self_probs(g, hs)
            given = mix_grad[at, hs]
            queries, keyed, valued = self_q[at, hs], self_k[at, hs], self_v[at, hs]
            prob_grad = dot_nt(given, valued)
            inner = jnp.sum(probs * prob_grad, axis=-1, keepdims=True)
            logit_grad = (probs * (prob_grad - inner)).astype(BF16)
            self_q[at, hs] = (dot_nn(logit_grad, keyed) * SCALE).astype(BF16)
            self_k[at, hs] = (dot_tn(logit_grad, queries) * SCALE).astype(BF16)
            self_v[at, hs] = dot_tn(probs.astype(BF16), given).astype(BF16)

    each(HEADS // 2, self_back)
    turn()
    each(HEADS // 2, lambda i: self_back(HEADS // 2 + i))
    turn()
    w = weights.use(S_Q)
    part[...] = dot_nt(self_q[...], w())
    w = weights.use(S_K)
    part[...] += dot_nt(self_k[...], w())
    w = weights.use(S_V)
    part[...] += dot_nt(self_v[...], w())

    def back_one(i):
        at = span_of(i)
        pull, gain_part, _ = norm_back(res_one[at, :], gain_of(2), part[at, :])
        total = grad[at, :] + pull
        grad[at, :] = total
        one_low[at, :] = total.astype(BF16)
        gain_add(2, gain_part)

    each(rows // tile, back_one)
    turn()

    def sum_groups(i):
        total = grad[span_of(i), :]
        for g in range(1, groups):
            total += grad[pl.ds(pl.multiple_of(g * LAT + i * tile, tile), tile), :]
        lat_grad[span_of(i), :] = total

    each(LAT // tile, sum_groups)
    w = weights.use(W_O)
    mix_grad[...] = dot_nt(one_low[...], w()).astype(BF16)

    def cross_back(h):
        hs = head_of(h)
        scores[...] = dot_nt(query[:, hs], keys[:, hs]) * SCALE
        for g in range(groups):
            res_two_view = dot_nt(mix_grad[group_of(g), hs], values[:, hs])
            part[pl.ds(0, LAT), :] = res_two_view[:, :half]
            part[pl.ds(LAT, LAT), :] = res_two_view[:, half:]

            def softmax_back(i, g=g):
                at = span_of(i, 32)
                row = pl.ds(pl.multiple_of(g * LAT + i * 32, 32), 32)
                here = lax.broadcasted_iota(jnp.int32, (32, HEAD), 1) == h
                total = jnp.sum(jnp.where(here, lse[row, :], 0.0), axis=-1, keepdims=True)
                low_row = pl.ds(pl.multiple_of(LAT + i * 32, 32), 32)
                prob_grads = (part[at, :], part[low_row, :])
                probs, inner = [], 0.0
                for side in range(2):
                    cols = pl.ds(side * half, half)
                    prob = jnp.exp(scores[at, cols] + count_log[pl.ds(g, 1), cols] - total)
                    wide[pl.ds(pl.multiple_of(side * rows + g * LAT + i * 32, 32), 32), :] = prob.astype(BF16)
                    inner += jnp.sum(prob * prob_grads[side], axis=-1, keepdims=True)
                    probs.append(prob)
                for side in range(2):
                    cols = pl.ds(side * half, half)
                    made = probs[side] * (prob_grads[side] - inner)
                    score_grad[at, cols] = made if g == 0 else score_grad[at, cols] + made

            each(LAT // 32, softmax_back)
        logit_grad = score_grad[...].astype(BF16)
        asked = query[:, hs]
        query_back = dot_nn(logit_grad, keys[:, hs]) * SCALE
        keys[:, hs] = (dot_tn(logit_grad, asked) * SCALE).astype(BF16)
        query[:, hs] = query_back.astype(BF16)
        for side in range(2):
            probs = wide[pl.ds(side * rows, rows), :]
            values[pl.ds(side * half, half), hs] = dot_tn(probs, mix_grad[:, hs]).astype(BF16)

    point_load.start()
    for part_at in range(4):
        each(2, lambda i, part_at=part_at: cross_back(part_at * 2 + i))
        turn(part_at < 3)

    w = weights.use(W_Q)
    pull, gain_part, _ = norm_back(lat[...], gain_of(0), dot_nt(query[...], w()))
    lat_grad[...] += pull
    gain_add(0, gain_part)

    point_load.wait()
    each(slots // tile, norm_points)
    turn()
    w_keys, w_values = weights.use(W_K), weights.use(W_V, keep=1)
    point_stores = []
    for block in range(slots // 512):
        at = pl.ds(block * 512, 512)
        part[...] = dot_nt(keys[at, :], w_keys()) + dot_nt(values[at, :], w_values())

        def back_points(i, block=block):
            row = pl.ds(pl.multiple_of(block * 512 + i * tile, tile), tile)
            pull, gain_part, _ = norm_back(slope[row, :].astype(F32), gain_of(1), part[span_of(i), :])
            slope[row, :] = pull.astype(BF16)
            gain_add(1, gain_part)

        each(512 // tile, back_points)
        store = pltpu.make_async_copy(slope.at[at], r["point_grad"].at[at], r["point_sem"].at[block])
        store.start()
        point_stores.append(store)
        if block < 2:
            turn()
    while len(getattr(reduce, "begun", ())) < len(QUEUE) and linked or not linked and reduce.count < len(QUEUE):
        turn()
    reduce.finish()
    for store in point_stores:
        store.wait()


def layer_call(linked, small, attn, up, down, points, near, lens, cot):
    slots, rows, groups = points.shape[0], cot.shape[0], near.shape[0]
    any_space = pl.BlockSpec(memory_space=pl.ANY)
    in_vmem = pl.BlockSpec(memory_space=pltpu.VMEM)
    in_smem = pl.BlockSpec(memory_space=pltpu.SMEM)
    shape = jax.ShapeDtypeStruct
    split = (2,) * 5
    outs = [shape((rows, D), BF16), shape((slots, D), BF16)]
    out_specs = [in_vmem, any_space]
    if linked:
        outs += [shape((PART, SMALL), F32)] + [shape((PART, D), F32)] * 8
        outs += [shape((QUARTERS, PART, D), F32), shape((QUARTERS * PART, D), F32)]
        out_specs += [any_space] * 11
        outs += [shape((CHUNKS, *split, PART, D), BF16), shape((*split, PART, SMALL), BF16)]
        out_specs += [any_space] * 2
    else:
        outs += [shape((D, SMALL), F32)] + [shape((D, D), BF16)] * 8
        outs += [shape((QUARTERS, D, D), BF16), shape((FF, D), BF16)]
        out_specs += [in_vmem] + [any_space] * 10
    vmem, dma = pltpu.VMEM, pltpu.SemaphoreType.DMA
    scratch = {
        "keys": vmem((slots, D), BF16),
        "values": vmem((slots, D), BF16),
        "wide": vmem((QUARTERS * rows, D), BF16),
        "slope": vmem((QUARTERS * rows, D), BF16),
    }
    for name in ("cross_mix", "self_mix", "h_s", "h_m", "self_q", "self_k", "self_v", "two_low", "one_low", "mix_grad"):
        scratch[name] = vmem((rows, D), BF16)
    for name in ("res_one", "res_two", "grad", "part"):
        scratch[name] = vmem((rows, D), F32)
    scratch |= {
        "scores": vmem((LAT, slots), F32),
        "score_grad": vmem((LAT, slots), F32),
        "lat": vmem((LAT, D), F32),
        "lat_grad": vmem((LAT, D), F32),
        "h_q": vmem((LAT, D), BF16),
        "query": vmem((LAT, D), BF16),
        "lse": vmem((rows, HEAD), F32),
        "gains": vmem((8, D), F32),
        "gain_grads": vmem((8, D), F32),
        "small_in": vmem((*split, PART, SMALL), BF16),
        "count_log": vmem((groups, slots), F32),
        "held": vmem((WEIGHT_SLOTS, *split, PART, D), BF16),
        "held_sem": dma((WEIGHT_SLOTS,)),
        "point_sem": dma((slots // 512,)),
        "tiny_sem": dma((1,)),
    }
    if linked:
        scratch["term"] = vmem((TERM_SLOTS, 2, 2, 2, 2, 2, PART, D), BF16)
        for stage in range(STAGES):
            scratch[f"land{stage}"] = vmem((LAND_SLOTS, *(2,) * (4 - stage), PART, D), BF16)
        pieces = 2 * CHUNKS + 1
        scratch |= {
            "final": vmem((2, PART, D), F32),
            "g_send": dma((pieces, STAGES)),
            "g_recv": dma((pieces, STAGES)),
            "own_sem": dma((CHUNKS + 1,)),
            "r_send": dma((len(QUEUE), STAGES, 3)),
            "r_recv": dma((len(QUEUE), STAGES, 3)),
            "credit": pltpu.SemaphoreType.REGULAR((STAGES, 3, 5)),
            "final_sem": dma((2,)),
        }
    else:
        scratch |= {"term": vmem((2, 512, D), BF16), "term_sem": dma((2,))}
    names = NAMES_IN + NAMES_OUT + (("full", "full_small") if linked else ()) + tuple(scratch)
    params = {"collective_id": 0} if linked else {}
    return pl.pallas_call(
        functools.partial(layer_kernel, linked, names),
        out_shape=outs,
        in_specs=[any_space] * 12 + [in_vmem, in_smem, in_vmem],
        out_specs=out_specs,
        scratch_shapes=list(scratch.values()),
        compiler_params=pltpu.CompilerParams(has_side_effects=True, vmem_limit_bytes=63 << 20, **params),
    )(small, *attn, up, down, points, near, lens, cot)


def on_device(
    linked, latents, gain_q, gain_kv, w_q, w_k, w_v, w_o, gain_s, s_q, s_k, s_v, s_o, gain_m, w_up, w_down,
    points, neighbours, lengths, cotangent,
):
    own = latents.shape[1]
    split = (2,) * 5
    small = jnp.concatenate((latents, jnp.stack((gain_q, gain_kv, gain_s, gain_m))), axis=0)
    small = jnp.pad(small.T, ((0, 0), (0, SMALL - LAT - 4)))
    attn = (w_k, w_v, w_q, w_o, s_q, s_k, s_v, s_o)
    if linked:
        up = w_up.reshape(own, PARTS, QUARTERS, PART).transpose(2, 0, 1, 3).reshape(QUARTERS, own, D)
        made = layer_call(True, small, attn, up, w_down, points, neighbours, lengths, cotangent)[: len(NAMES_OUT)]
        out, point_grad, g_small, g_k, g_v, g_q, g_o, gs_q, gs_k, gs_v, gs_o, g_up, g_down = made
        g_up = g_up.reshape(QUARTERS, own, PARTS, PART).transpose(1, 2, 0, 3).reshape(own, FF)
    else:
        gathered = lambda shard: lax.all_gather(shard, AXES, axis=0, tiled=True)
        blocks = lambda whole: whole.reshape(*split, PART, whole.shape[-1])
        up = gathered(w_up).reshape(D, QUARTERS, D).transpose(1, 0, 2).reshape(QUARTERS, *split, PART, D)
        down = gathered(w_down).reshape(QUARTERS, *split, PART, D)
        made = layer_call(
            False, blocks(gathered(small)), [blocks(gathered(one)) for one in attn], up, down,
            points, neighbours, lengths, cotangent,
        )
        out, point_grad = made[:2]
        summed = lambda whole: lax.psum_scatter(whole.astype(F32), AXES, scatter_dimension=0, tiled=True)
        g_small, g_k, g_v, g_q, g_o, gs_q, gs_k, gs_v, gs_o = [summed(one) for one in made[2:11]]
        g_up = summed(made[11].transpose(1, 0, 2).reshape(D, FF))
        g_down = summed(made[12])
    turned = g_small.T
    return (
        out, point_grad, turned[:LAT], turned[LAT], turned[LAT + 1], g_q, g_k, g_v, g_o,
        turned[LAT + 2], gs_q, gs_k, gs_v, gs_o, turned[LAT + 3], g_up, g_down,
    )


def solution(mesh):
    linked = (mesh.shape["dp"], mesh.shape["fsdp"]) == LINKED_MESH
    row, vector, matrix = P(None, AXES), P(AXES), P(AXES, None)
    return jax.shard_map(
        functools.partial(on_device, linked),
        mesh=mesh,
        in_specs=(
            row, vector, vector, matrix, matrix, matrix, matrix, vector, matrix, matrix, matrix, matrix, vector,
            matrix, matrix, matrix, matrix, vector, matrix,
        ),
        out_specs=(
            matrix, matrix, row, vector, vector, matrix, matrix, matrix, matrix,
            vector, matrix, matrix, matrix, matrix, vector, matrix, matrix,
        ),
        check_vma=False,
    )
```

```python
import functools

import jax
import jax.numpy as jnp
from jax import lax
from jax.experimental import pallas as pl
from jax.experimental.pallas import tpu as pltpu
from jax.sharding import PartitionSpec as P

HEADS = 8
HEAD = 128
D = 1024
FF = 4096
LAT = 128
NEIGH = 512

EPSILON = 1e-05
MASK_FILL = -1e30
SCALE = HEAD**-0.5
LOG2_E = 1.4426950408889634
GELU_K = 0.7978845608028654
GELU_C = 0.044715

AXES = ("dp", "fsdp")
MESH = pl.DeviceIdType.MESH
F32 = jnp.float32
BF16 = jnp.bfloat16

LINKED_MESH = (4, 8)
PARTS = 32
PART = D // PARTS
SMALL = 256
QUARTERS = FF // D

W_K, W_V, W_Q, W_O, S_Q, S_K, S_V, S_O, UP, DOWN = 0, 1, 2, 3, 4, 5, 6, 7, 8, 12
CHUNKS = 16
TINY = CHUNKS

Y, X, ZH, ZL, CORE = range(5)
STAGES = 5
GATHER_ORDERS = ((ZL, ZH, X, Y, CORE), (ZL, ZH, Y, X, CORE), (ZH, X, Y, ZL, CORE), (ZH, Y, X, ZL, CORE))
GATHER_MIX = (0, 1, 2, 0, 1, 3)
GATHER_LAG = 3
REDUCE_ORDERS = tuple(tuple(reversed(order)) for order in GATHER_ORDERS)
REDUCE_LAG = 2
LAND_SLOTS = 4
TERM_SLOTS = 2
WEIGHT_SLOTS = 2
LOADS = tuple(range(CHUNKS)) + tuple(range(UP, DOWN)) + (S_O, S_Q, S_K, S_V, W_O, W_Q, W_K, W_V)
QUEUE = tuple(range(DOWN, CHUNKS)) + tuple(range(UP, DOWN)) + (S_O, S_Q, S_K, S_V, W_O, W_K, W_V, W_Q, TINY)


def dot_nn(left, right):
    return jnp.dot(left, right, preferred_element_type=F32)


def dot_nt(left, right):
    return lax.dot_general(left, right, (((1,), (1,)), ((), ())), preferred_element_type=F32)


def dot_tn(left, right):
    return lax.dot_general(left, right, (((0,), (0,)), ((), ())), preferred_element_type=F32)


def row_mean(rows):
    return jnp.mean(rows, axis=-1, keepdims=True)


def normalised(rows):
    centred = rows - row_mean(rows)
    inv = lax.rsqrt(row_mean(centred * centred) + EPSILON)
    return centred * inv, inv


def norm_back(rows, gain, grad):
    unit, inv = normalised(rows)
    scaled = grad * gain
    pull = inv * (scaled - row_mean(scaled) - unit * row_mean(scaled * unit))
    return pull, jnp.sum(grad * unit, axis=0, keepdims=True), unit


def bits_of():
    row, col = lax.axis_index("dp"), lax.axis_index("fsdp")
    return (row // 2, row % 2, col // 4, (col // 2) % 2, col % 2)


def across(bits, axis):
    other = [1 - bit if at == axis else bit for at, bit in enumerate(bits)]
    return (other[Y] * 2 + other[X], other[ZH] * 4 + other[ZL] * 2 + other[CORE])


def swap_matrix():
    deal = lax.broadcasted_iota(jnp.int32, (512, 512), 0)
    take = lax.broadcasted_iota(jnp.int32, (512, 512), 1)
    same = (deal // 128 == take // 32 % 4) & (deal // 32 % 4 == take // 128) & (deal % 32 == take % 32)
    return jnp.where(same, 1.0, 0.0).astype(BF16)


class Gather:
    def __init__(self, refs, bits):
        self.refs, self.bits = refs, bits
        self.pieces = [(TINY, 0, PART, GATHER_ORDERS[0])]
        for chunk in range(CHUNKS):
            for half in range(2):
                order = GATHER_ORDERS[GATHER_MIX[(2 * chunk + half) % len(GATHER_MIX)]]
                self.pieces.append((chunk, half * (PART // 2), PART // 2, order))
        self.ticks = len(self.pieces) + STAGES * GATHER_LAG
        self.now, self.done = 0, 0

    def shard(self, chunk, row, rows):
        if chunk == TINY:
            return self.refs["small"].at[pl.ds(row, rows)]
        return self.refs["res_low"].at[pl.ds(chunk * PART + row, rows)]

    def place(self, chunk, index, row, rows):
        if chunk == TINY:
            return self.refs["full_small"].at[(*index, pl.ds(row, rows))]
        return self.refs["full"].at[(chunk, *index, pl.ds(row, rows))]

    def own_copy(self, chunk):
        return pltpu.make_async_copy(
            self.shard(chunk, 0, PART), self.place(chunk, self.bits, 0, PART), self.refs["own_sem"].at[chunk]
        )

    def copy(self, piece, stage):
        chunk, row, rows, order = self.pieces[piece]
        if stage == 0:
            source, target = self.shard(chunk, row, rows), self.place(chunk, self.bits, row, rows)
        else:
            index = [pl.ds(0, 2) if axis in order[:stage] else self.bits[axis] for axis in range(5)]
            source = target = self.place(chunk, index, row, rows)
        return pltpu.make_async_remote_copy(
            src_ref=source,
            dst_ref=target,
            send_sem=self.refs["g_send"].at[piece, stage],
            recv_sem=self.refs["g_recv"].at[piece, stage],
            device_id=across(self.bits, order[stage]),
            device_id_type=MESH,
        )

    def tick(self):
        if self.now >= self.ticks:
            return
        for stage in range(STAGES, -1, -1):
            piece = self.now - stage * GATHER_LAG
            if not 0 <= piece < len(self.pieces):
                continue
            chunk, row = self.pieces[piece][:2]
            if stage == 0 and row == 0:
                self.own_copy(chunk).start()
            if stage == 1 and row == 0:
                self.own_copy(chunk).wait()
            if stage > 0:
                self.copy(piece, stage - 1).wait_recv()
            if stage < STAGES:
                self.copy(piece, stage).start()
            else:
                self.done = piece + 1
        self.now += 1

    def has(self, chunk):
        return self.done > (0 if chunk == TINY else 2 * chunk + 2)

    def need(self, chunk):
        while not self.has(chunk):
            self.tick()

    def finish(self):
        while self.now < self.ticks:
            self.tick()
        for piece in range(len(self.pieces)):
            for stage in range(STAGES):
                self.copy(piece, stage).wait_send()


class Reduce:
    def __init__(self, refs, bits):
        self.refs, self.bits = refs, bits
        self.lands = [refs[f"land{stage}"] for stage in range(STAGES)]
        self.now, self.begun = 0, []

    def pieces(self, at):
        if QUEUE[at] == TINY:
            return [(0, 0, SMALL, REDUCE_ORDERS[0])]
        return [(0, 0, 384, REDUCE_ORDERS[0]), (1, 384, 384, REDUCE_ORDERS[1]), (2, 768, 256, REDUCE_ORDERS[2 + at % 2])]

    def open_axes(self, order, stage):
        return [axis for axis in range(5) if axis not in order[: stage + 1]]

    def kept(self, order, stage, spot):
        return [self.bits[one] if one == order[stage] else spot(one) for one in self.open_axes(order, stage - 1)]

    def copy(self, at, stage, piece):
        number, col, cols, order = piece
        slot, span = at % LAND_SLOTS, pl.ds(col, cols)
        every = pl.ds(0, 2)
        if stage == 0:
            source = self.refs["term"].at[(at % TERM_SLOTS, 1 - self.bits[CORE], *[every] * 4, pl.ds(0, PART), span)]
        else:
            index = [
                1 - self.bits[one] if one == order[stage] else every for one in self.open_axes(order, stage - 1)
            ]
            source = self.lands[stage - 1].at[(slot, *index, pl.ds(0, PART), span)]
        target = self.lands[stage].at[(slot, *[every] * (4 - stage), pl.ds(0, PART), span)]
        return pltpu.make_async_remote_copy(
            src_ref=source,
            dst_ref=target,
            send_sem=self.refs["r_send"].at[at, stage, number],
            recv_sem=self.refs["r_recv"].at[at, stage, number],
            device_id=across(self.bits, order[stage]),
            device_id_type=MESH,
        )

    def credit(self, stage, number, axis):
        return self.refs["credit"].at[stage, number, axis]

    def release(self, at, stage):
        later = at + LAND_SLOTS
        if later >= len(QUEUE):
            return
        for number, _, _, order in self.pieces(later):
            axis = order[stage]
            pl.semaphore_signal(
                self.credit(stage, number, axis), inc=1, device_id=across(self.bits, axis), device_id_type=MESH
            )

    def send(self, at, stage):
        for piece in self.pieces(at):
            if at >= LAND_SLOTS:
                pl.semaphore_wait(self.credit(stage, piece[0], piece[3][stage]), 1)
            self.copy(at, stage, piece).start()

    def add(self, at, stage, piece):
        number, col, cols, order = piece
        slot, span, land = at % LAND_SLOTS, pl.ds(col, cols), self.lands[stage]
        left = self.open_axes(order, stage)

        def step(i, carry):
            index = [(i >> (len(left) - 1 - k)) & 1 for k in range(len(left))]
            if stage == 0:
                extra = self.refs["term"][(at % TERM_SLOTS, self.bits[CORE], *index, slice(None), span)]
            else:
                kept = self.kept(order, stage, dict(zip(left, index)).get)
                extra = self.lands[stage - 1][(slot, *kept, slice(None), span)]
            land[(slot, *index, slice(None), span)] += extra
            return carry

        lax.fori_loop(0, 1 << len(left), step, 0)

    def advance(self, at, stage):
        assert stage < STAGES or self.refs["freed"]
        pieces = self.pieces(at)
        last = stage == STAGES
        slot = at % LAND_SLOTS
        if last:
            self.final_ready(at)
        for piece in pieces:
            self.copy(at, stage - 1, piece).wait_recv()
        if stage == 1:
            self.add(at, 0, (0, 0, SMALL if QUEUE[at] == TINY else D, pieces[0][3]))
        else:
            for piece in pieces:
                if last:
                    _, col, cols, order = piece
                    span = pl.ds(col, cols)
                    mine = self.lands[3][(slot, *self.kept(order, 4, None), slice(None), span)]
                    came = self.lands[4][slot, :, span]
                    total = mine.astype(F32) + came.astype(F32)
                    if UP <= QUEUE[at] < DOWN:
                        self.refs["up_sum"][pl.ds((QUEUE[at] - UP) * PART, PART), span] = total
                    else:
                        self.refs["final"][pl.ds(at % 2 * PART, PART), span] = total
                else:
                    self.add(at, stage - 1, piece)
        if last and QUEUE[at] == DOWN - 1:
            self.restore_up()
        if last and (QUEUE[at] < UP or QUEUE[at] >= DOWN):
            self.final_copy(at).start()
        if not last:
            self.send(at, stage)
        for piece in pieces:
            self.copy(at, stage - 1, piece).wait_send()
        if stage >= 2:
            self.release(at, stage - 2)
        if last:
            self.release(at, 4)

    def final_copy(self, at):
        chunk = QUEUE[at]
        source, sem = self.refs["final"].at[pl.ds(at % 2 * PART, PART)], self.refs["final_sem"].at[at % 2]
        if chunk == TINY:
            source, target = source.at[:, pl.ds(0, SMALL)], self.refs["g_small"]
        elif chunk < UP:
            target = self.refs["g_attn"][chunk]
        else:
            target = self.refs["g_down"].at[pl.ds((chunk - DOWN) * PART, PART)]
        return pltpu.make_async_copy(source, target, sem)

    def final_ready(self, at):
        if at >= 2 and not UP <= QUEUE[at - 2] < DOWN:
            self.final_copy(at - 2).wait()

    def up_copy(self, quarter):
        return pltpu.make_async_copy(
            self.refs["res_two"].at[pl.ds(quarter * PART, PART)],
            self.refs["g_up"].at[:, pl.ds(quarter * D, D)],
            self.refs["final_sem"].at[2 + quarter],
        )

    def restore_up(self):
        rows = [
            jnp.concatenate([self.refs["up_sum"][pl.ds(q * PART, PART), pl.ds(i * 128, 128)] for q in range(QUARTERS)], axis=1)
            for i in range(8)
        ]
        rows = jnp.concatenate(rows, axis=0)
        swap = swap_matrix()
        top = rows.astype(BF16)
        rest = rows - top.astype(F32)
        mid = rest.astype(BF16)
        low = (rest - mid.astype(F32)).astype(BF16)
        back = dot_nn(top, swap) + dot_nn(mid, swap) + dot_nn(low, swap)
        for i in range(8):
            spot = (pl.ds(i // 2 * PART, PART), pl.ds(i % 2 * 512, 512))
            self.refs["res_two"][spot] = back[i * PART : (i + 1) * PART]
        for quarter in range(QUARTERS):
            self.up_copy(quarter).start()

    def tick(self, tile):
        for at, began in enumerate(self.begun):
            stage, between = divmod(self.now - began, REDUCE_LAG)
            if between == 0 and 1 <= stage <= STAGES:
                self.advance(at, stage)
        if tile is not None and len(self.begun) < len(QUEUE):
            at = len(self.begun)
            width = SMALL if QUEUE[at] == TINY else D
            for i in range(2):
                value = tile(QUEUE[at], i).astype(BF16).reshape(8, 2, PART, width)
                for core in range(2):
                    for j in range(8):
                        index = (at % TERM_SLOTS, core, i, j >> 2, (j >> 1) & 1, j & 1, slice(None), pl.ds(0, width))
                        self.refs["term"][index] = value[j, core]
            self.send(at, 0)
            self.begun.append(self.now)
        self.now += 1

    def finish(self):
        assert len(self.begun) == len(QUEUE)
        while self.now - self.begun[-1] <= STAGES * REDUCE_LAG:
            self.tick(None)
        for at in (len(QUEUE) - 2, len(QUEUE) - 1):
            self.final_copy(at).wait()
        for quarter in range(QUARTERS):
            self.up_copy(quarter).wait()


class Local:
    def __init__(self, refs):
        self.refs, self.count, self.tiles = refs, 0, 0

    def copy(self, tile):
        chunk, half = QUEUE[tile // 2], tile % 2
        rows = pl.ds(half * 512, 512)
        if chunk < UP:
            target = self.refs["g_attn"][chunk].at[rows]
        elif chunk < DOWN:
            target = self.refs["g_up"].at[chunk - UP, rows]
        else:
            target = self.refs["g_down"].at[pl.ds((chunk - DOWN) * D + half * 512, 512)]
        return pltpu.make_async_copy(self.refs["term"].at[half], target, self.refs["term_sem"].at[half])

    def tick(self, tile):
        if tile is None or self.count >= len(QUEUE):
            return
        chunk = QUEUE[self.count]
        self.count += 1
        for half in range(2):
            value = tile(chunk, half)
            if chunk == TINY:
                self.refs["g_small"][pl.ds(half * 512, 512), :] = value
                continue
            if self.tiles >= 2:
                self.copy(self.tiles - 2).wait()
            self.refs["term"][half] = value.astype(BF16)
            self.copy(self.tiles).start()
            self.tiles += 1

    def finish(self):
        assert self.count == len(QUEUE)
        for tile in (self.tiles - 2, self.tiles - 1):
            self.copy(tile).wait()


class Weights:
    def __init__(self, refs, gather):
        self.refs, self.gather = refs, gather
        self.fetched, self.used = 0, 0

    def copy(self, at):
        chunk = LOADS[at]
        if self.gather is not None:
            source = self.refs["full"].at[chunk]
        elif chunk < UP:
            source = self.refs["attn"][chunk]
        elif chunk < DOWN:
            source = self.refs["up"].at[chunk - UP]
        else:
            source = self.refs["down"].at[chunk - DOWN]
        slot = at % WEIGHT_SLOTS
        return pltpu.make_async_copy(source, self.refs["held"].at[slot], self.refs["held_sem"].at[slot])

    def fetch(self, limit):
        while self.fetched < min(limit, len(LOADS)):
            if self.gather is not None:
                self.gather.need(LOADS[self.fetched])
            self.copy(self.fetched).start()
            self.fetched += 1

    def ready(self, at):
        return at >= CHUNKS or self.gather is None or self.gather.has(LOADS[at])

    def use(self, chunk, keep=0):
        at = self.used
        assert LOADS[at] == chunk
        self.fetch(at + 1)
        while self.fetched < min(at + WEIGHT_SLOTS - keep, len(LOADS)) and self.ready(self.fetched):
            self.fetch(self.fetched + 1)
        self.copy(at).wait()
        self.used += 1
        return lambda: self.refs["held"][at % WEIGHT_SLOTS].reshape(D, D)


NAMES_IN = ("small", "w_k", "w_v", "w_q", "w_o", "s_q", "s_k", "s_v", "s_o", "up", "down", "points", "near", "lens", "cot")
NAMES_OUT = ("out", "point_grad", "g_small", "g_k", "g_v", "g_q", "g_o", "gs_q", "gs_k", "gs_v", "gs_o", "g_up", "g_down")


def layer_kernel(linked, names, *refs):
    r = dict(zip(names, refs, strict=True))
    r["attn"] = [r[name] for name in NAMES_IN[1:9]]
    r["freed"] = False
    r["g_attn"] = [r[name] for name in NAMES_OUT[3:11]]
    r["up_sum"] = r["res_two"].at[pl.ds(QUARTERS * PART, QUARTERS * PART)]
    r["final"] = r["res_two"].at[pl.ds(2 * QUARTERS * PART, 2 * PART)]
    r["lat_grad"] = r["res_two"].at[pl.ds(3 * QUARTERS * PART, LAT)]
    points, near, lens, cot = r["points"], r["near"], r["lens"], r["cot"]
    keys, values, wide, slope = r["keys"], r["values"], r["wide"], r["slope"]
    cross_mix, self_mix, h_s, h_m = r["cross_mix"], r["self_mix"], r["h_s"], r["h_m"]
    self_q, self_k, self_v = r["self_q"], r["self_k"], r["self_v"]
    res_low, mix_grad = r["res_low"], r["mix_grad"]
    res_one, res_two, grad, part = r["res_one"], r["res_two"], r["grad"], r["part"]
    lat, lat_grad = r["lat"], r["lat_grad"]
    h_q, query, lse, gains, gain_grads = r["h_q"], r["query"], r["lse"], r["gains"], r["gain_grads"]
    count_log = r["count_log"]
    groups = near.shape[0]
    rows, slots = cot.shape[0], keys.shape[0]
    half = slots // 2

    if linked:
        bits = bits_of()
        barrier = pltpu.get_barrier_semaphore()
        for axis in range(5):
            pl.semaphore_signal(barrier, inc=1, device_id=across(bits, axis), device_id_type=MESH)
        pl.semaphore_wait(barrier, 5)
        gather, reduce = Gather(r, bits), Reduce(r, bits)
        move = gather.tick
    else:
        gather, reduce = None, Local(r)
        move = lambda: None
    weights = Weights(r, gather)

    point_load = pltpu.make_async_copy(points, slope, r["point_sem"].at[0])
    point_load.start()
    own_rows = r["res_low"]
    if linked:
        own_loads = [
            pltpu.make_async_copy(ref, own_rows.at[pl.ds(chunk * PART, PART)], r["own_sem"].at[chunk])
            for chunk, ref in enumerate(r["attn"])
        ]
        own_loads.append(
            pltpu.make_async_copy(r["down"], own_rows.at[pl.ds(DOWN * PART, QUARTERS * PART)], r["own_sem"].at[DOWN])
        )
        for load in own_loads:
            load.start()
        for load in own_loads:
            load.wait()
    for _ in range(6):
        move()
    if linked:
        tall = jnp.concatenate([r["up"][:, pl.ds(i * 512, 512)] for i in range(8)], axis=0)
        dealt = dot_nn(tall, swap_matrix()).astype(BF16)
        for i in range(8):
            for q in range(QUARTERS):
                own_rows[pl.ds((UP + q) * PART, PART), pl.ds(i * 128, 128)] = dealt[i * PART : (i + 1) * PART, q * 128 : (q + 1) * 128]
    move()
    move()

    for g in range(groups):
        listed = near[pl.ds(g, 1), :]
        live = lax.broadcasted_iota(jnp.int32, (1, NEIGH), 1) < lens[g]
        high = lax.broadcasted_iota(jnp.int32, (slots // 128, NEIGH), 0) == listed // 128
        low = lax.broadcasted_iota(jnp.int32, (128, NEIGH), 0) == listed % 128
        high = jnp.where(high & live, 1.0, 0.0).astype(BF16)
        low = jnp.where(low, 1.0, 0.0).astype(BF16)
        count = dot_nt(high, low)
        count = jnp.where(count > 0.5, jnp.log2(jnp.maximum(count, 1.0)), MASK_FILL)
        for a in range(slots // 128):
            count_log[pl.ds(g, 1), pl.ds(a * 128, 128)] = count[a : a + 1, :]

    small_in = r["held"].at[(1, *[pl.ds(0, 2)] * 5, pl.ds(0, PART), pl.ds(0, SMALL))]
    if linked:
        gather.need(TINY)
        small_load = pltpu.make_async_copy(r["full_small"], small_in, r["tiny_sem"].at[0])
    else:
        small_load = pltpu.make_async_copy(r["small"], small_in, r["tiny_sem"].at[0])
    small_load.start()
    small_load.wait()
    turned = small_in[...].reshape(D, SMALL).astype(F32).T
    lat[...] = turned[:LAT]
    gains[...] = turned[LAT : LAT + 8]
    gain_grads[...] = jnp.zeros_like(gain_grads)
    gain_of = lambda i: gains[pl.ds(i, 1), :]
    h_q[...] = (normalised(lat[...])[0] * gain_of(0)).astype(BF16)
    point_load.wait()

    tile = 64

    def span_of(i, size=tile):
        return pl.ds(pl.multiple_of(i * size, size), size)

    def head_of(h):
        return pl.ds(pl.multiple_of(h * HEAD, HEAD), HEAD)

    def each(count, step, unroll=1):
        def body(i, carry):
            step(i)
            return carry

        lax.fori_loop(0, count, body, 0, unroll=unroll)

    def norm_points(i):
        at = span_of(i)
        wide[at, :] = (normalised(slope[at, :].astype(F32))[0] * gain_of(1)).astype(BF16)

    each(slots // tile, norm_points, 4)

    for chunk, target in ((W_K, keys), (W_V, values)):
        w = weights.use(chunk)

        def project(i, target=target, w=w):
            at = span_of(i, 512)
            target[at, :] = dot_nn(wide[at, :], w()).astype(BF16)

        each(slots // 512, project)
        move()
        move()
    w = weights.use(W_Q)
    query[...] = dot_nn(h_q[...], w()).astype(BF16)

    def weigh(h):
        hs = head_of(h)
        logits = dot_nt(query[:, hs], keys[:, hs]) * (SCALE * LOG2_E)
        here = lax.broadcasted_iota(jnp.int32, (LAT, HEAD), 1) == h
        for g in range(groups):
            logit = logits + count_log[pl.ds(g, 1), :]
            top = jnp.max(logit, axis=-1, keepdims=True)
            terms = jnp.exp2(logit - top)
            total = jnp.sum(terms, axis=-1, keepdims=True)
            probs = (terms * (1.0 / total)).astype(BF16)
            row = pl.ds(g * LAT, LAT)
            wide[row, :] = probs[:, :half]
            wide[pl.ds(rows + g * LAT, LAT), :] = probs[:, half:]
            lse[row, :] = jnp.where(here, top + jnp.log2(total), lse[row, :])
        mixed = dot_nn(wide[pl.ds(0, rows), :], values[pl.ds(0, half), hs])
        mixed += dot_nn(wide[pl.ds(rows, rows), :], values[pl.ds(half, half), hs])
        cross_mix[:, hs] = mixed.astype(BF16)

    lse[...] = jnp.zeros_like(lse)
    for part_at in range(4):
        each(2, lambda i, part_at=part_at: weigh(part_at * 2 + i))
        move()
        move()

    w = weights.use(W_O)
    res_one[...] = dot_nn(cross_mix[...], w())

    def add_latents(i):
        at = span_of(i)
        total = res_one[at, :] + lat[span_of(i % (LAT // tile)), :]
        res_one[at, :] = total
        h_s[at, :] = (normalised(total)[0] * gain_of(2)).astype(BF16)

    each(rows // tile, add_latents, 4)
    for chunk, target in ((S_Q, self_q), (S_K, self_k), (S_V, self_v)):
        w = weights.use(chunk)
        target[...] = dot_nn(h_s[...], w()).astype(BF16)

    def group_of(g):
        return pl.ds(g * LAT, LAT)

    def self_probs(g, hs):
        logit = dot_nt(self_q[group_of(g), hs], self_k[group_of(g), hs]) * SCALE
        terms = jnp.exp(logit - jnp.max(logit, axis=-1, keepdims=True))
        return terms * (1.0 / jnp.sum(terms, axis=-1, keepdims=True))

    def self_attend(h):
        hs = head_of(h)
        for g in range(groups):
            probs = self_probs(g, hs).astype(BF16)
            self_mix[group_of(g), hs] = dot_nn(probs, self_v[group_of(g), hs]).astype(BF16)

    for part_at in range(2):
        each(HEADS // 2, lambda i, part_at=part_at: self_attend(part_at * 4 + i), 2)
        move()
    w = weights.use(S_O)
    res_two[...] = dot_nn(self_mix[...], w())

    def add_first(i):
        at = span_of(i)
        total = res_two[at, :] + res_one[at, :]
        res_two[at, :] = total
        h_m[at, :] = (normalised(total)[0] * gain_of(3)).astype(BF16)

    each(rows // tile, add_first, 4)

    def quarter(q):
        return pl.ds(q * rows, rows)

    def terms_of(chunk, i):
        cols = pl.ds(i * 512, 512)
        if chunk == TINY:
            tall = jnp.concatenate((lat_grad[...], gain_grads[...], jnp.zeros((SMALL - LAT - 8, D), F32)), axis=0)
            return tall[:, i * 512 : (i + 1) * 512].T
        if chunk >= DOWN:
            q = chunk - DOWN
            return dot_tn(wide[quarter(q), cols], cot[...])
        if chunk >= UP:
            return dot_tn(h_m[:, cols], slope[quarter(chunk - UP), :])
        left, right = {
            S_O: (self_mix, res_low),
            S_Q: (h_s, self_q),
            S_K: (h_s, self_k),
            S_V: (h_s, self_v),
            W_O: (cross_mix, res_low),
            W_K: (wide, keys),
            W_V: (wide, values),
            W_Q: (h_q, query),
        }[chunk]
        return dot_tn(left[:, cols], right[...])

    def turn(fresh=True):
        reduce.tick(terms_of if fresh else None)

    for q in range(QUARTERS):
        w = weights.use(UP + q)

        def expand(i, q=q, w=w):
            u = dot_nn(h_m[span_of(i, 256), :], w())
            square = u * u
            bent = jnp.tanh(GELU_K * (u + GELU_C * square * u))
            at = pl.ds(pl.multiple_of(q * rows + i * 256, 256), 256)
            wide[at, :] = (0.5 * u * (1.0 + bent)).astype(BF16)
            rise = GELU_K * (1.0 + 3.0 * GELU_C * square)
            slope[at, :] = (0.5 * (1.0 + bent) + 0.5 * u * (1.0 - bent * bent) * rise).astype(BF16)

        each(rows // 256, expand)
        turn()

    for q in range(QUARTERS):
        w = weights.use(DOWN + q)
        made = dot_nn(wide[quarter(q), :], w())
        part[...] = made + (res_two[...] if q == 0 else part[...])
        act_grad = dot_nt(cot[...], w())
        slope[quarter(q), :] = (slope[quarter(q), :].astype(F32) * act_grad).astype(BF16)
        turn()
    mix_grad[...] = part[...].astype(BF16)
    out_store = pltpu.make_async_copy(mix_grad, r["out"], r["tiny_sem"].at[1])
    out_store.start()
    if linked:
        gather.finish()

    for q in range(QUARTERS):
        w = weights.use(UP + q)
        made = dot_nt(slope[quarter(q), :], w())
        grad[...] = made if q == 0 else grad[...] + made
        if q % 2 == 1:
            turn(False)

    def gain_add(i, value):
        gain_grads[pl.ds(i, 1), :] += value

    def back_two(i):
        at = span_of(i)
        pull, gain_part, _ = norm_back(res_two[at, :], gain_of(3), grad[at, :])
        total = cot[at, :].astype(F32) + pull
        grad[at, :] = total
        res_low[at, :] = total.astype(BF16)
        gain_add(3, gain_part)

    each(rows // tile, back_two, 2)
    r["freed"] = True
    turn()
    w = weights.use(S_O)
    out_store.wait()
    mix_grad[...] = dot_nt(res_low[...], w()).astype(BF16)

    def self_back(h):
        hs = head_of(h)
        for g in range(groups):
            at = group_of(g)
            probs = self_probs(g, hs)
            given = mix_grad[at, hs]
            queries, keyed, valued = self_q[at, hs], self_k[at, hs], self_v[at, hs]
            prob_grad = dot_nt(given, valued)
            inner = jnp.sum(self_mix[at, hs].astype(F32) * given.astype(F32), axis=-1, keepdims=True)
            logit_grad = (probs * (prob_grad - inner)).astype(BF16)
            self_q[at, hs] = (dot_nn(logit_grad, keyed) * SCALE).astype(BF16)
            self_k[at, hs] = (dot_tn(logit_grad, queries) * SCALE).astype(BF16)
            self_v[at, hs] = dot_tn(probs.astype(BF16), given).astype(BF16)

    each(HEADS // 2, self_back, 2)
    turn(False)
    each(HEADS // 2, lambda i: self_back(HEADS // 2 + i), 2)
    turn()
    w = weights.use(S_Q)
    part[...] = dot_nt(self_q[...], w())
    w = weights.use(S_K)
    part[...] += dot_nt(self_k[...], w())
    w = weights.use(S_V)
    part[...] += dot_nt(self_v[...], w())
    turn()

    def back_one(i):
        at = span_of(i)
        pull, gain_part, _ = norm_back(res_one[at, :], gain_of(2), part[at, :])
        total = grad[at, :] + pull
        grad[at, :] = total
        res_low[at, :] = total.astype(BF16)
        gain_add(2, gain_part)

    each(rows // tile, back_one, 2)
    turn()

    def sum_groups(i):
        total = grad[span_of(i), :]
        for g in range(1, groups):
            total += grad[pl.ds(pl.multiple_of(g * LAT + i * tile, tile), tile), :]
        lat_grad[span_of(i), :] = total

    each(LAT // tile, sum_groups)
    w = weights.use(W_O)
    mix_grad[...] = dot_nt(res_low[...], w()).astype(BF16)
    turn()

    def cross_back(h):
        hs = head_of(h)
        logits = dot_nt(query[:, hs], keys[:, hs]) * (SCALE * LOG2_E)
        here = lax.broadcasted_iota(jnp.int32, (LAT, HEAD), 1) == h
        made = None
        for g in range(groups):
            at = group_of(g)
            given = mix_grad[at, hs]
            prob_grad = dot_nt(given, values[:, hs])
            total = jnp.sum(jnp.where(here, lse[at, :], 0.0), axis=-1, keepdims=True)
            inner = jnp.sum(cross_mix[at, hs].astype(F32) * given.astype(F32), axis=-1, keepdims=True)
            probs = jnp.exp2(logits + count_log[pl.ds(g, 1), :] - total)
            low = probs.astype(BF16)
            wide[at, :] = low[:, :half]
            wide[pl.ds(rows + g * LAT, LAT), :] = low[:, half:]
            pulled = probs * (prob_grad - inner)
            made = pulled if g == 0 else made + pulled
        logit_grad = made.astype(BF16)
        asked = query[:, hs]
        query_back = dot_nn(logit_grad, keys[:, hs]) * SCALE
        keys[:, hs] = (dot_tn(logit_grad, asked) * SCALE).astype(BF16)
        query[:, hs] = query_back.astype(BF16)
        for side in range(2):
            probs = wide[pl.ds(side * rows, rows), :]
            values[pl.ds(side * half, half), hs] = dot_tn(probs, mix_grad[:, hs]).astype(BF16)

    point_load.start()
    for part_at in range(4):
        each(2, lambda i, part_at=part_at: cross_back(part_at * 2 + i))
        turn(False)

    w = weights.use(W_Q)
    pull, gain_part, _ = norm_back(lat[...], gain_of(0), dot_nt(query[...], w()))
    lat_grad[...] += pull
    gain_add(0, gain_part)

    point_load.wait()
    each(slots // tile, norm_points, 4)
    turn()
    w_keys, w_values = weights.use(W_K), weights.use(W_V, keep=1)
    point_stores = []
    for block in range(slots // 512):
        at = pl.ds(block * 512, 512)
        part[...] = dot_nt(keys[at, :], w_keys()) + dot_nt(values[at, :], w_values())

        def back_points(i, block=block):
            row = pl.ds(pl.multiple_of(block * 512 + i * tile, tile), tile)
            pull, gain_part, _ = norm_back(slope[row, :].astype(F32), gain_of(1), part[span_of(i), :])
            slope[row, :] = pull.astype(BF16)
            gain_add(1, gain_part)

        each(512 // tile, back_points, 2)
        store = pltpu.make_async_copy(slope.at[at], r["point_grad"].at[at], r["point_sem"].at[block])
        store.start()
        point_stores.append(store)
        turn(block < 2)
    while len(getattr(reduce, "begun", ())) < len(QUEUE) and linked or not linked and reduce.count < len(QUEUE):
        turn()
    reduce.finish()
    for store in point_stores:
        store.wait()


def layer_call(linked, small, attn, up, down, points, near, lens, cot):
    slots, rows, groups = points.shape[0], cot.shape[0], near.shape[0]
    any_space = pl.BlockSpec(memory_space=pl.ANY)
    in_vmem = pl.BlockSpec(memory_space=pltpu.VMEM)
    in_smem = pl.BlockSpec(memory_space=pltpu.SMEM)
    shape = jax.ShapeDtypeStruct
    split = (2,) * 5
    outs = [shape((rows, D), BF16), shape((slots, D), BF16)]
    out_specs = [any_space, any_space]
    if linked:
        outs += [shape((PART, SMALL), F32)] + [shape((PART, D), F32)] * 8
        outs += [shape((PART, FF), F32), shape((QUARTERS * PART, D), F32)]
        out_specs += [any_space] * 11
        outs += [shape((CHUNKS, *split, PART, D), BF16), shape((*split, PART, SMALL), BF16)]
        out_specs += [any_space] * 2
    else:
        outs += [shape((D, SMALL), F32)] + [shape((D, D), BF16)] * 8
        outs += [shape((QUARTERS, D, D), BF16), shape((FF, D), BF16)]
        out_specs += [in_vmem] + [any_space] * 10
    vmem, dma = pltpu.VMEM, pltpu.SemaphoreType.DMA
    scratch = {
        "keys": vmem((slots, D), BF16),
        "values": vmem((slots, D), BF16),
        "wide": vmem((QUARTERS * rows, D), BF16),
        "slope": vmem((QUARTERS * rows, D), BF16),
    }
    for name in ("cross_mix", "self_mix", "h_s", "h_m", "self_q", "self_k", "self_v", "res_low", "mix_grad"):
        scratch[name] = vmem((rows, D), BF16)
    for name in ("res_one", "res_two", "grad", "part"):
        scratch[name] = vmem((rows, D), F32)
    scratch |= {
        "lat": vmem((LAT, D), F32),
        "h_q": vmem((LAT, D), BF16),
        "query": vmem((LAT, D), BF16),
        "lse": vmem((rows, HEAD), F32),
        "gains": vmem((8, D), F32),
        "gain_grads": vmem((8, D), F32),
        "count_log": vmem((groups, slots), F32),
        "held": vmem((WEIGHT_SLOTS, *split, PART, D), BF16),
        "held_sem": dma((WEIGHT_SLOTS,)),
        "point_sem": dma((slots // 512,)),
        "tiny_sem": dma((2,)),
    }
    if linked:
        scratch["term"] = vmem((TERM_SLOTS, 2, 2, 2, 2, 2, PART, D), BF16)
        for stage in range(STAGES):
            scratch[f"land{stage}"] = vmem((LAND_SLOTS, *(2,) * (4 - stage), PART, D), BF16)
        pieces = 2 * CHUNKS + 1
        scratch |= {
            "g_send": dma((pieces, STAGES)),
            "g_recv": dma((pieces, STAGES)),
            "own_sem": dma((CHUNKS + 1,)),
            "r_send": dma((len(QUEUE), STAGES, 3)),
            "r_recv": dma((len(QUEUE), STAGES, 3)),
            "credit": pltpu.SemaphoreType.REGULAR((STAGES, 3, 5)),
            "final_sem": dma((2 + QUARTERS,)),
        }
    else:
        scratch |= {"term": vmem((2, 512, D), BF16), "term_sem": dma((2,))}
    names = NAMES_IN + NAMES_OUT + (("full", "full_small") if linked else ()) + tuple(scratch)
    params = {"collective_id": 0} if linked else {}
    return pl.pallas_call(
        functools.partial(layer_kernel, linked, names),
        out_shape=outs,
        in_specs=[in_vmem if linked else any_space] + [any_space] * 8 + [in_vmem if linked else any_space] + [any_space] * 2 + [in_vmem, in_smem, in_vmem],
        out_specs=out_specs,
        scratch_shapes=list(scratch.values()),
        compiler_params=pltpu.CompilerParams(has_side_effects=True, vmem_limit_bytes=63 << 20, **params),
    )(small, *attn, up, down, points, near, lens, cot)


HAND_ROWS = 512


def hand_over_kernel(count, small, *refs):
    sources, (lat_out, *targets) = refs[:count], refs[count : 2 * count + 1]
    gains = refs[2 * count + 1 : 2 * count + 5]
    stages, load_sem, store_sem = refs[2 * count + 5 : -2], refs[-2], refs[-1]
    loads, stores = [], []
    for source, target, stage in zip(sources, targets, stages, strict=True):
        for row in range(0, source.shape[0], HAND_ROWS):
            at, i = pl.ds(row, min(HAND_ROWS, source.shape[0])), len(loads)
            loads.append(pltpu.make_async_copy(source.at[at], stage.at[at], load_sem.at[i]))
            stores.append(pltpu.make_async_copy(stage.at[at], target.at[at], store_sem.at[i]))
    for load in loads:
        load.start()
    lat_out[...] = small[:, pl.ds(0, LAT)]
    turned = small[...].T
    for i, gain in enumerate(gains):
        gain[...] = turned[LAT + i : LAT + i + 1]
    for load, store in zip(loads, stores, strict=True):
        load.wait()
        store.start()
    for store in stores:
        store.wait()


def hand_over(made):
    out, point_grad, small, *grads = made
    moved = [point_grad, out, *grads]
    any_space = pl.BlockSpec(memory_space=pl.ANY)
    in_vmem = pl.BlockSpec(memory_space=pltpu.VMEM)
    own = small.shape[0]
    count = sum(max(one.shape[0] // HAND_ROWS, 1) for one in moved)
    lat_out, point_grad, out, *rest = pl.pallas_call(
        functools.partial(hand_over_kernel, len(moved)),
        out_shape=[jax.ShapeDtypeStruct((own, LAT), F32)]
        + [jax.ShapeDtypeStruct(one.shape, one.dtype) for one in moved]
        + [jax.ShapeDtypeStruct((1, own), F32)] * 4,
        in_specs=[in_vmem] + [any_space] * len(moved),
        out_specs=[in_vmem] + [any_space] * len(moved) + [in_vmem] * 4,
        scratch_shapes=[pltpu.VMEM(one.shape, one.dtype) for one in moved]
        + [pltpu.SemaphoreType.DMA((count,))] * 2,
        compiler_params=pltpu.CompilerParams(vmem_limit_bytes=60 << 20),
    )(small, *moved)
    return (out, point_grad, lat_out, *rest)


def on_device(
    linked, latents, gain_q, gain_kv, w_q, w_k, w_v, w_o, gain_s, s_q, s_k, s_v, s_o, gain_m, w_up, w_down,
    points, neighbours, lengths, cotangent,
):
    split = (2,) * 5
    lane = lax.broadcasted_iota(jnp.int32, (1, SMALL), 1)
    small = jnp.pad(latents.T, ((0, 0), (0, SMALL - LAT)))
    for i, gain in enumerate((gain_q, gain_kv, gain_s, gain_m)):
        small = jnp.where(lane == LAT + i, gain[:, None], small)
    attn = (w_k, w_v, w_q, w_o, s_q, s_k, s_v, s_o)
    if linked:
        made = layer_call(True, small, attn, w_up, w_down, points, neighbours, lengths, cotangent)[: len(NAMES_OUT)]
        out, point_grad, turned, g_k, g_v, g_q, g_o, gs_q, gs_k, gs_v, gs_o, g_up, g_down, *gains = hand_over(made)
        turned = turned.T
        gains = [gain.reshape(-1) for gain in gains]
    else:
        gathered = lambda shard: lax.all_gather(shard, AXES, axis=0, tiled=True)
        blocks = lambda whole: whole.reshape(*split, PART, whole.shape[-1])
        up = gathered(w_up).reshape(D, QUARTERS, D).transpose(1, 0, 2).reshape(QUARTERS, *split, PART, D)
        down = gathered(w_down).reshape(QUARTERS, *split, PART, D)
        made = layer_call(
            False, blocks(gathered(small)), [blocks(gathered(one)) for one in attn], up, down,
            points, neighbours, lengths, cotangent,
        )
        out, point_grad = made[:2]
        summed = lambda whole: lax.psum_scatter(whole.astype(F32), AXES, scatter_dimension=0, tiled=True)
        g_small, g_k, g_v, g_q, g_o, gs_q, gs_k, gs_v, gs_o = [summed(one) for one in made[2:11]]
        g_up = summed(made[11].transpose(1, 0, 2).reshape(D, FF))
        g_down = summed(made[12])
        turned = g_small.T[:LAT]
        gains = [g_small[:, LAT + i] for i in range(4)]
    return (
        out, point_grad, turned, gains[0], gains[1], g_q, g_k, g_v, g_o,
        gains[2], gs_q, gs_k, gs_v, gs_o, gains[3], g_up, g_down,
    )


def solution(mesh):
    linked = (mesh.shape["dp"], mesh.shape["fsdp"]) == LINKED_MESH
    row, vector, matrix = P(None, AXES), P(AXES), P(AXES, None)
    return jax.shard_map(
        functools.partial(on_device, linked),
        mesh=mesh,
        in_specs=(
            row, vector, vector, matrix, matrix, matrix, matrix, vector, matrix, matrix, matrix, matrix, vector,
            matrix, matrix, matrix, matrix, vector, matrix,
        ),
        out_specs=(
            matrix, matrix, row, vector, vector, matrix, matrix, matrix, matrix,
            vector, matrix, matrix, matrix, matrix, vector, matrix, matrix,
        ),
        check_vma=False,
    )
```

```python
import functools

import jax
import jax.numpy as jnp
from jax import lax
from jax.experimental import pallas as pl
from jax.experimental.pallas import tpu as pltpu
from jax.sharding import PartitionSpec as P

HEADS = 8
HEAD = 128
D = 1024
FF = 4096
LAT = 128
NEIGH = 512

EPSILON = 1e-05
MASK_FILL = -1e30
SCALE = HEAD**-0.5
LOG2_E = 1.4426950408889634
GELU_K = 0.7978845608028654
GELU_C = 0.044715

AXES = ("dp", "fsdp")
MESH = pl.DeviceIdType.MESH
F32 = jnp.float32
BF16 = jnp.bfloat16

LINKED_MESH = (4, 8)
PARTS = 32
PART = D // PARTS
SMALL = 256
QUARTERS = FF // D

W_K, W_V, W_Q, W_O, S_Q, S_K, S_V, S_O, UP, DOWN = 0, 1, 2, 3, 4, 5, 6, 7, 8, 12
CHUNKS = 16
TINY = CHUNKS

Y, X, ZH, ZL, CORE = range(5)
STAGES = 5
GATHER_ORDERS = ((ZL, ZH, X, Y, CORE), (ZL, ZH, Y, X, CORE), (ZH, X, Y, ZL, CORE), (ZH, Y, X, ZL, CORE))
GATHER_MIX = (0, 1, 2, 0, 1, 3)
GATHER_LAG = 3
REDUCE_ORDERS = tuple(tuple(reversed(order)) for order in GATHER_ORDERS)
REDUCE_LAG = 2
LAND_SLOTS = 4
TERM_SLOTS = 2
WEIGHT_SLOTS = 2
LOADS = tuple(range(CHUNKS)) + tuple(range(UP, DOWN)) + (S_O, S_Q, S_K, S_V, W_O, W_Q, W_K, W_V)
QUEUE = tuple(range(DOWN, CHUNKS)) + tuple(range(UP, DOWN)) + (S_O, S_Q, S_K, S_V, W_O, W_K, W_V, W_Q, TINY)


def dot_nn(left, right):
    return jnp.dot(left, right, preferred_element_type=F32)


def dot_nt(left, right):
    return lax.dot_general(left, right, (((1,), (1,)), ((), ())), preferred_element_type=F32)


def dot_tn(left, right):
    return lax.dot_general(left, right, (((0,), (0,)), ((), ())), preferred_element_type=F32)


def row_mean(rows):
    return jnp.mean(rows, axis=-1, keepdims=True)


def normalised(rows):
    centred = rows - row_mean(rows)
    inv = lax.rsqrt(row_mean(centred * centred) + EPSILON)
    return centred * inv, inv


def norm_back(rows, gain, grad):
    unit, inv = normalised(rows)
    scaled = grad * gain
    pull = inv * (scaled - row_mean(scaled) - unit * row_mean(scaled * unit))
    return pull, jnp.sum(grad * unit, axis=0, keepdims=True), unit


def bits_of():
    row, col = lax.axis_index("dp"), lax.axis_index("fsdp")
    return (row // 2, row % 2, col // 4, (col // 2) % 2, col % 2)


def across(bits, axis):
    other = [1 - bit if at == axis else bit for at, bit in enumerate(bits)]
    return (other[Y] * 2 + other[X], other[ZH] * 4 + other[ZL] * 2 + other[CORE])


def swap_matrix():
    deal = lax.broadcasted_iota(jnp.int32, (512, 512), 0)
    take = lax.broadcasted_iota(jnp.int32, (512, 512), 1)
    same = (deal // 128 == take // 32 % 4) & (deal // 32 % 4 == take // 128) & (deal % 32 == take % 32)
    return jnp.where(same, 1.0, 0.0).astype(BF16)


class Gather:
    def __init__(self, refs, bits):
        self.refs, self.bits = refs, bits
        self.pieces = [(TINY, 0, PART, GATHER_ORDERS[0])]
        for chunk in range(CHUNKS):
            for half in range(2):
                order = GATHER_ORDERS[GATHER_MIX[(2 * chunk + half) % len(GATHER_MIX)]]
                self.pieces.append((chunk, half * (PART // 2), PART // 2, order))
        self.ticks = len(self.pieces) + STAGES * GATHER_LAG
        self.now, self.done = 0, 0

    def shard(self, chunk, row, rows):
        if chunk == TINY:
            return self.refs["small"].at[pl.ds(row, rows)]
        return self.refs["res_low"].at[pl.ds(chunk * PART + row, rows)]

    def place(self, chunk, index, row, rows):
        if chunk == TINY:
            return self.refs["full_small"].at[(*index, pl.ds(row, rows))]
        return self.refs["full"].at[(chunk, *index, pl.ds(row, rows))]

    def own_copy(self, chunk):
        return pltpu.make_async_copy(
            self.shard(chunk, 0, PART), self.place(chunk, self.bits, 0, PART), self.refs["own_sem"].at[chunk]
        )

    def copy(self, piece, stage):
        chunk, row, rows, order = self.pieces[piece]
        if stage == 0:
            source, target = self.shard(chunk, row, rows), self.place(chunk, self.bits, row, rows)
        else:
            index = [pl.ds(0, 2) if axis in order[:stage] else self.bits[axis] for axis in range(5)]
            source = target = self.place(chunk, index, row, rows)
        return pltpu.make_async_remote_copy(
            src_ref=source,
            dst_ref=target,
            send_sem=self.refs["g_send"].at[piece, stage],
            recv_sem=self.refs["g_recv"].at[piece, stage],
            device_id=across(self.bits, order[stage]),
            device_id_type=MESH,
        )

    def tick(self):
        if self.now >= self.ticks:
            return
        for stage in (0, *range(STAGES, 0, -1)):
            piece = self.now - stage * GATHER_LAG
            if not 0 <= piece < len(self.pieces):
                continue
            chunk, row = self.pieces[piece][:2]
            if stage == 0 and row == 0:
                self.own_copy(chunk).start()
            if stage == 1 and row == 0:
                self.own_copy(chunk).wait()
            if stage > 0:
                self.copy(piece, stage - 1).wait_recv()
            if stage < STAGES:
                self.copy(piece, stage).start()
            else:
                self.done = piece + 1
        self.now += 1

    def has(self, chunk):
        return self.done > (0 if chunk == TINY else 2 * chunk + 2)

    def need(self, chunk):
        while not self.has(chunk):
            self.tick()

    def finish(self):
        while self.now < self.ticks:
            self.tick()
        for piece in range(len(self.pieces)):
            for stage in range(STAGES):
                self.copy(piece, stage).wait_send()


class Reduce:
    def __init__(self, refs, bits):
        self.refs, self.bits = refs, bits
        self.lands = [refs[f"land{stage}"] for stage in range(STAGES)]
        self.now, self.begun = 0, []

    def pieces(self, at):
        if QUEUE[at] == TINY:
            return [(0, 0, SMALL, REDUCE_ORDERS[0])]
        return [(0, 0, 384, REDUCE_ORDERS[0]), (1, 384, 384, REDUCE_ORDERS[1]), (2, 768, 256, REDUCE_ORDERS[2 + at % 2])]

    def open_axes(self, order, stage):
        return [axis for axis in range(5) if axis not in order[: stage + 1]]

    def kept(self, order, stage, spot):
        return [self.bits[one] if one == order[stage] else spot(one) for one in self.open_axes(order, stage - 1)]

    def copy(self, at, stage, piece):
        number, col, cols, order = piece
        slot, span = at % LAND_SLOTS, pl.ds(col, cols)
        every = pl.ds(0, 2)
        if stage == 0:
            source = self.refs["term"].at[(at % TERM_SLOTS, 1 - self.bits[CORE], *[every] * 4, pl.ds(0, PART), span)]
        else:
            index = [
                1 - self.bits[one] if one == order[stage] else every for one in self.open_axes(order, stage - 1)
            ]
            source = self.lands[stage - 1].at[(slot, *index, pl.ds(0, PART), span)]
        target = self.lands[stage].at[(slot, *[every] * (4 - stage), pl.ds(0, PART), span)]
        return pltpu.make_async_remote_copy(
            src_ref=source,
            dst_ref=target,
            send_sem=self.refs["r_send"].at[at, stage, number],
            recv_sem=self.refs["r_recv"].at[at, stage, number],
            device_id=across(self.bits, order[stage]),
            device_id_type=MESH,
        )

    def credit(self, stage, number, axis):
        return self.refs["credit"].at[stage, number, axis]

    def release(self, at, stage):
        later = at + LAND_SLOTS
        if later >= len(QUEUE):
            return
        for number, _, _, order in self.pieces(later):
            axis = order[stage]
            pl.semaphore_signal(
                self.credit(stage, number, axis), inc=1, device_id=across(self.bits, axis), device_id_type=MESH
            )

    def send(self, at, stage):
        for piece in self.pieces(at):
            if at >= LAND_SLOTS:
                pl.semaphore_wait(self.credit(stage, piece[0], piece[3][stage]), 1)
            self.copy(at, stage, piece).start()

    def add(self, at, stage, piece):
        number, col, cols, order = piece
        slot, span, land = at % LAND_SLOTS, pl.ds(col, cols), self.lands[stage]
        left = self.open_axes(order, stage)

        def step(i, carry):
            index = [(i >> (len(left) - 1 - k)) & 1 for k in range(len(left))]
            if stage == 0:
                extra = self.refs["term"][(at % TERM_SLOTS, self.bits[CORE], *index, slice(None), span)]
            else:
                kept = self.kept(order, stage, dict(zip(left, index)).get)
                extra = self.lands[stage - 1][(slot, *kept, slice(None), span)]
            land[(slot, *index, slice(None), span)] += extra
            return carry

        lax.fori_loop(0, 1 << len(left), step, 0)

    def advance(self, at, stage):
        assert stage < STAGES or self.refs["freed"]
        pieces = self.pieces(at)
        last = stage == STAGES
        slot = at % LAND_SLOTS
        if last:
            self.final_ready(at)
        for piece in pieces:
            self.copy(at, stage - 1, piece).wait_recv()
        if stage == 1:
            self.add(at, 0, (0, 0, SMALL if QUEUE[at] == TINY else D, pieces[0][3]))
        else:
            for piece in pieces:
                if last:
                    _, col, cols, order = piece
                    span = pl.ds(col, cols)
                    mine = self.lands[3][(slot, *self.kept(order, 4, None), slice(None), span)]
                    came = self.lands[4][slot, :, span]
                    total = mine.astype(F32) + came.astype(F32)
                    if UP <= QUEUE[at] < DOWN:
                        self.refs["up_sum"][pl.ds((QUEUE[at] - UP) * PART, PART), span] = total
                    else:
                        self.refs["final"][pl.ds(at % 2 * PART, PART), span] = total
                else:
                    self.add(at, stage - 1, piece)
        if last and QUEUE[at] == DOWN - 1:
            self.restore_up()
        if last and (QUEUE[at] < UP or QUEUE[at] >= DOWN):
            self.final_copy(at).start()
        if not last:
            self.send(at, stage)
        for piece in pieces:
            self.copy(at, stage - 1, piece).wait_send()
        if stage >= 2:
            self.release(at, stage - 2)
        if last:
            self.release(at, 4)

    def final_copy(self, at):
        chunk = QUEUE[at]
        source, sem = self.refs["final"].at[pl.ds(at % 2 * PART, PART)], self.refs["final_sem"].at[at % 2]
        if chunk == TINY:
            source, target = source.at[:, pl.ds(0, SMALL)], self.refs["g_small"]
        elif chunk < UP:
            target = self.refs["g_attn"][chunk]
        else:
            target = self.refs["g_down"].at[pl.ds((chunk - DOWN) * PART, PART)]
        return pltpu.make_async_copy(source, target, sem)

    def final_ready(self, at):
        if at >= 2 and not UP <= QUEUE[at - 2] < DOWN:
            self.final_copy(at - 2).wait()

    def up_copy(self, quarter):
        return pltpu.make_async_copy(
            self.refs["res_two"].at[pl.ds(quarter * PART, PART)],
            self.refs["g_up"].at[:, pl.ds(quarter * D, D)],
            self.refs["final_sem"].at[2 + quarter],
        )

    def restore_up(self):
        rows = [
            jnp.concatenate([self.refs["up_sum"][pl.ds(q * PART, PART), pl.ds(i * 128, 128)] for q in range(QUARTERS)], axis=1)
            for i in range(8)
        ]
        rows = jnp.concatenate(rows, axis=0)
        swap = swap_matrix()
        top = rows.astype(BF16)
        rest = rows - top.astype(F32)
        mid = rest.astype(BF16)
        low = (rest - mid.astype(F32)).astype(BF16)
        back = dot_nn(top, swap) + dot_nn(mid, swap) + dot_nn(low, swap)
        for i in range(8):
            spot = (pl.ds(i // 2 * PART, PART), pl.ds(i % 2 * 512, 512))
            self.refs["res_two"][spot] = back[i * PART : (i + 1) * PART]
        for quarter in range(QUARTERS):
            self.up_copy(quarter).start()

    def tick(self, tile):
        for at, began in enumerate(self.begun):
            stage, between = divmod(self.now - began, REDUCE_LAG)
            if between == 0 and 1 <= stage <= STAGES:
                self.advance(at, stage)
        if tile is not None and len(self.begun) < len(QUEUE):
            at = len(self.begun)
            width = SMALL if QUEUE[at] == TINY else D
            for i in range(2):
                value = tile(QUEUE[at], i).astype(BF16).reshape(8, 2, PART, width)
                for core in range(2):
                    for j in range(8):
                        index = (at % TERM_SLOTS, core, i, j >> 2, (j >> 1) & 1, j & 1, slice(None), pl.ds(0, width))
                        self.refs["term"][index] = value[j, core]
            self.send(at, 0)
            self.begun.append(self.now)
        self.now += 1

    def finish(self):
        assert len(self.begun) == len(QUEUE)
        while self.now - self.begun[-1] <= STAGES * REDUCE_LAG:
            self.tick(None)
        for at in (len(QUEUE) - 2, len(QUEUE) - 1):
            self.final_copy(at).wait()
        for quarter in range(QUARTERS):
            self.up_copy(quarter).wait()


class Local:
    def __init__(self, refs):
        self.refs, self.count, self.tiles = refs, 0, 0

    def copy(self, tile):
        chunk, half = QUEUE[tile // 2], tile % 2
        rows = pl.ds(half * 512, 512)
        if chunk < UP:
            target = self.refs["g_attn"][chunk].at[rows]
        elif chunk < DOWN:
            target = self.refs["g_up"].at[chunk - UP, rows]
        else:
            target = self.refs["g_down"].at[pl.ds((chunk - DOWN) * D + half * 512, 512)]
        return pltpu.make_async_copy(self.refs["term"].at[half], target, self.refs["term_sem"].at[half])

    def tick(self, tile):
        if tile is None or self.count >= len(QUEUE):
            return
        chunk = QUEUE[self.count]
        self.count += 1
        for half in range(2):
            value = tile(chunk, half)
            if chunk == TINY:
                self.refs["g_small"][pl.ds(half * 512, 512), :] = value
                continue
            if self.tiles >= 2:
                self.copy(self.tiles - 2).wait()
            self.refs["term"][half] = value.astype(BF16)
            self.copy(self.tiles).start()
            self.tiles += 1

    def finish(self):
        assert self.count == len(QUEUE)
        for tile in (self.tiles - 2, self.tiles - 1):
            self.copy(tile).wait()


class Weights:
    def __init__(self, refs, gather):
        self.refs, self.gather = refs, gather
        self.fetched, self.used = 0, 0

    def copy(self, at):
        chunk = LOADS[at]
        if self.gather is not None:
            source = self.refs["full"].at[chunk]
        elif chunk < UP:
            source = self.refs["attn"][chunk]
        elif chunk < DOWN:
            source = self.refs["up"].at[chunk - UP]
        else:
            source = self.refs["down"].at[chunk - DOWN]
        slot = at % WEIGHT_SLOTS
        return pltpu.make_async_copy(source, self.refs["held"].at[slot], self.refs["held_sem"].at[slot])

    def fetch(self, limit):
        while self.fetched < min(limit, len(LOADS)):
            if self.gather is not None:
                self.gather.need(LOADS[self.fetched])
            self.copy(self.fetched).start()
            self.fetched += 1

    def ready(self, at):
        return at >= CHUNKS or self.gather is None or self.gather.has(LOADS[at])

    def use(self, chunk, keep=0):
        at = self.used
        assert LOADS[at] == chunk
        self.fetch(at + 1)
        while self.fetched < min(at + WEIGHT_SLOTS - keep, len(LOADS)) and self.ready(self.fetched):
            self.fetch(self.fetched + 1)
        self.copy(at).wait()
        self.used += 1
        return lambda: self.refs["held"][at % WEIGHT_SLOTS].reshape(D, D)


NAMES_IN = ("small", "w_k", "w_v", "w_q", "w_o", "s_q", "s_k", "s_v", "s_o", "up", "down", "points", "near", "lens", "cot")
NAMES_OUT = ("out", "point_grad", "g_small", "g_k", "g_v", "g_q", "g_o", "gs_q", "gs_k", "gs_v", "gs_o", "g_up", "g_down")


def layer_kernel(linked, names, *refs):
    r = dict(zip(names, refs, strict=True))
    r["attn"] = [r[name] for name in NAMES_IN[1:9]]
    r["freed"] = False
    r["g_attn"] = [r[name] for name in NAMES_OUT[3:11]]
    r["up_sum"] = r["res_two"].at[pl.ds(QUARTERS * PART, QUARTERS * PART)]
    r["final"] = r["res_two"].at[pl.ds(2 * QUARTERS * PART, 2 * PART)]
    r["lat_grad"] = r["res_two"].at[pl.ds(3 * QUARTERS * PART, LAT)]
    points, near, lens, cot = r["points"], r["near"], r["lens"], r["cot"]
    keys, values, wide, slope = r["keys"], r["values"], r["wide"], r["slope"]
    cross_mix, self_mix, h_s, h_m = r["cross_mix"], r["self_mix"], r["h_s"], r["h_m"]
    self_q, self_k, self_v = r["self_q"], r["self_k"], r["self_v"]
    res_low, mix_grad = r["res_low"], r["mix_grad"]
    res_one, res_two, grad, part = r["res_one"], r["res_two"], r["grad"], r["part"]
    lat, lat_grad = r["lat"], r["lat_grad"]
    h_q, query, lse, gains, gain_grads = r["h_q"], r["query"], r["lse"], r["gains"], r["gain_grads"]
    count_log = r["count_log"]
    groups = near.shape[0]
    rows, slots = cot.shape[0], keys.shape[0]
    half = slots // 2

    if linked:
        bits = bits_of()
        barrier = pltpu.get_barrier_semaphore()
        for axis in range(5):
            pl.semaphore_signal(barrier, inc=1, device_id=across(bits, axis), device_id_type=MESH)
        pl.semaphore_wait(barrier, 5)
        gather, reduce = Gather(r, bits), Reduce(r, bits)
        move = gather.tick
    else:
        gather, reduce = None, Local(r)
        move = lambda: None
    weights = Weights(r, gather)

    point_load = pltpu.make_async_copy(points, slope, r["point_sem"].at[0])
    point_load.start()
    own_rows = r["res_low"]
    if linked:
        own_loads = [
            pltpu.make_async_copy(ref, own_rows.at[pl.ds(chunk * PART, PART)], r["own_sem"].at[chunk])
            for chunk, ref in enumerate(r["attn"])
        ]
        own_loads.append(
            pltpu.make_async_copy(r["down"], own_rows.at[pl.ds(DOWN * PART, QUARTERS * PART)], r["own_sem"].at[DOWN])
        )
        for load in own_loads:
            load.start()
        for load in own_loads:
            load.wait()
    for _ in range(6):
        move()
    if linked:
        tall = jnp.concatenate([r["up"][:, pl.ds(i * 512, 512)] for i in range(8)], axis=0)
        dealt = dot_nn(tall, swap_matrix()).astype(BF16)
        for i in range(8):
            for q in range(QUARTERS):
                own_rows[pl.ds((UP + q) * PART, PART), pl.ds(i * 128, 128)] = dealt[i * PART : (i + 1) * PART, q * 128 : (q + 1) * 128]
    move()
    move()

    for g in range(groups):
        listed = near[pl.ds(g, 1), :]
        live = lax.broadcasted_iota(jnp.int32, (1, NEIGH), 1) < lens[g]
        high = lax.broadcasted_iota(jnp.int32, (slots // 128, NEIGH), 0) == listed // 128
        low = lax.broadcasted_iota(jnp.int32, (128, NEIGH), 0) == listed % 128
        high = jnp.where(high & live, 1.0, 0.0).astype(BF16)
        low = jnp.where(low, 1.0, 0.0).astype(BF16)
        count = dot_nt(high, low)
        count = jnp.where(count > 0.5, jnp.log2(jnp.maximum(count, 1.0)), MASK_FILL)
        for a in range(slots // 128):
            count_log[pl.ds(g, 1), pl.ds(a * 128, 128)] = count[a : a + 1, :]

    small_in = r["held"].at[(1, *[pl.ds(0, 2)] * 5, pl.ds(0, PART), pl.ds(0, SMALL))]
    if linked:
        gather.need(TINY)
        small_load = pltpu.make_async_copy(r["full_small"], small_in, r["tiny_sem"].at[0])
    else:
        small_load = pltpu.make_async_copy(r["small"], small_in, r["tiny_sem"].at[0])
    small_load.start()
    small_load.wait()
    turned = small_in[...].reshape(D, SMALL).astype(F32).T
    lat[...] = turned[:LAT]
    gains[...] = turned[LAT : LAT + 8]
    gain_grads[...] = jnp.zeros_like(gain_grads)
    gain_of = lambda i: gains[pl.ds(i, 1), :]
    h_q[...] = (normalised(lat[...])[0] * gain_of(0)).astype(BF16)
    point_load.wait()

    tile = 64

    def span_of(i, size=tile):
        return pl.ds(pl.multiple_of(i * size, size), size)

    def head_of(h):
        return pl.ds(pl.multiple_of(h * HEAD, HEAD), HEAD)

    def each(count, step, unroll=1):
        def body(i, carry):
            step(i)
            return carry

        lax.fori_loop(0, count, body, 0, unroll=unroll)

    def norm_points(i):
        at = span_of(i)
        wide[at, :] = (normalised(slope[at, :].astype(F32))[0] * gain_of(1)).astype(BF16)

    each(slots // tile, norm_points, 4)

    for chunk, target in ((W_K, keys), (W_V, values)):
        w = weights.use(chunk)

        def project(i, target=target, w=w):
            at = span_of(i, 512)
            target[at, :] = dot_nn(wide[at, :], w()).astype(BF16)

        each(slots // 512, project)
        move()
        move()
    w = weights.use(W_Q)
    query[...] = dot_nn(h_q[...], w()).astype(BF16)

    def weigh(h):
        hs = head_of(h)
        logits = dot_nt(query[:, hs], keys[:, hs]) * (SCALE * LOG2_E)
        here = lax.broadcasted_iota(jnp.int32, (LAT, HEAD), 1) == h
        for g in range(groups):
            logit = logits + count_log[pl.ds(g, 1), :]
            top = jnp.max(logit, axis=-1, keepdims=True)
            terms = jnp.exp2(logit - top)
            total = jnp.sum(terms, axis=-1, keepdims=True)
            probs = (terms * (1.0 / total)).astype(BF16)
            row = pl.ds(g * LAT, LAT)
            wide[row, :] = probs[:, :half]
            wide[pl.ds(rows + g * LAT, LAT), :] = probs[:, half:]
            lse[row, :] = jnp.where(here, top + jnp.log2(total), lse[row, :])
        mixed = dot_nn(wide[pl.ds(0, rows), :], values[pl.ds(0, half), hs])
        mixed += dot_nn(wide[pl.ds(rows, rows), :], values[pl.ds(half, half), hs])
        cross_mix[:, hs] = mixed.astype(BF16)

    lse[...] = jnp.zeros_like(lse)
    for part_at in range(4):
        each(2, lambda i, part_at=part_at: weigh(part_at * 2 + i))
        move()
        move()

    w = weights.use(W_O)
    res_one[...] = dot_nn(cross_mix[...], w())

    def add_latents(i):
        at = span_of(i)
        total = res_one[at, :] + lat[span_of(i % (LAT // tile)), :]
        res_one[at, :] = total
        h_s[at, :] = (normalised(total)[0] * gain_of(2)).astype(BF16)

    each(rows // tile, add_latents, 4)
    for chunk, target in ((S_Q, self_q), (S_K, self_k), (S_V, self_v)):
        w = weights.use(chunk)
        target[...] = dot_nn(h_s[...], w()).astype(BF16)

    def group_of(g):
        return pl.ds(g * LAT, LAT)

    def self_probs(g, hs):
        logit = dot_nt(self_q[group_of(g), hs], self_k[group_of(g), hs]) * SCALE
        terms = jnp.exp(logit - jnp.max(logit, axis=-1, keepdims=True))
        return terms * (1.0 / jnp.sum(terms, axis=-1, keepdims=True))

    def self_attend(h):
        hs = head_of(h)
        for g in range(groups):
            probs = self_probs(g, hs).astype(BF16)
            self_mix[group_of(g), hs] = dot_nn(probs, self_v[group_of(g), hs]).astype(BF16)

    for part_at in range(2):
        each(HEADS // 2, lambda i, part_at=part_at: self_attend(part_at * 4 + i), 2)
        move()
    w = weights.use(S_O)
    res_two[...] = dot_nn(self_mix[...], w())

    def add_first(i):
        at = span_of(i)
        total = res_two[at, :] + res_one[at, :]
        res_two[at, :] = total
        h_m[at, :] = (normalised(total)[0] * gain_of(3)).astype(BF16)

    each(rows // tile, add_first, 4)

    def quarter(q):
        return pl.ds(q * rows, rows)

    def terms_of(chunk, i):
        cols = pl.ds(i * 512, 512)
        if chunk == TINY:
            tall = jnp.concatenate((lat_grad[...], gain_grads[...], jnp.zeros((SMALL - LAT - 8, D), F32)), axis=0)
            return tall[:, i * 512 : (i + 1) * 512].T
        if chunk >= DOWN:
            q = chunk - DOWN
            return dot_tn(wide[quarter(q), cols], cot[...])
        if chunk >= UP:
            return dot_tn(h_m[:, cols], slope[quarter(chunk - UP), :])
        left, right = {
            S_O: (self_mix, res_low),
            S_Q: (h_s, self_q),
            S_K: (h_s, self_k),
            S_V: (h_s, self_v),
            W_O: (cross_mix, res_low),
            W_K: (wide, keys),
            W_V: (wide, values),
            W_Q: (h_q, query),
        }[chunk]
        return dot_tn(left[:, cols], right[...])

    def turn(fresh=True):
        reduce.tick(terms_of if fresh else None)

    for q in range(QUARTERS):
        w = weights.use(UP + q)

        def expand(i, q=q, w=w):
            u = dot_nn(h_m[span_of(i, 256), :], w())
            square = u * u
            bent = jnp.tanh(GELU_K * (u + GELU_C * square * u))
            at = pl.ds(pl.multiple_of(q * rows + i * 256, 256), 256)
            wide[at, :] = (0.5 * u * (1.0 + bent)).astype(BF16)
            rise = GELU_K * (1.0 + 3.0 * GELU_C * square)
            slope[at, :] = (0.5 * (1.0 + bent) + 0.5 * u * (1.0 - bent * bent) * rise).astype(BF16)

        each(rows // 256, expand)
        turn()

    for q in range(QUARTERS):
        w = weights.use(DOWN + q)
        made = dot_nn(wide[quarter(q), :], w())
        part[...] = made + (res_two[...] if q == 0 else part[...])
        act_grad = dot_nt(cot[...], w())
        slope[quarter(q), :] = (slope[quarter(q), :].astype(F32) * act_grad).astype(BF16)
        turn()
    mix_grad[...] = part[...].astype(BF16)
    out_store = pltpu.make_async_copy(mix_grad, r["out"], r["tiny_sem"].at[1])
    out_store.start()
    if linked:
        gather.finish()

    for q in range(QUARTERS):
        w = weights.use(UP + q)
        made = dot_nt(slope[quarter(q), :], w())
        grad[...] = made if q == 0 else grad[...] + made
        if q % 2 == 1:
            turn(False)

    def gain_add(i, value):
        gain_grads[pl.ds(i, 1), :] += value

    def back_two(i):
        at = span_of(i)
        pull, gain_part, _ = norm_back(res_two[at, :], gain_of(3), grad[at, :])
        total = cot[at, :].astype(F32) + pull
        grad[at, :] = total
        res_low[at, :] = total.astype(BF16)
        gain_add(3, gain_part)

    each(rows // tile, back_two, 2)
    r["freed"] = True
    turn()
    w = weights.use(S_O)
    out_store.wait()
    mix_grad[...] = dot_nt(res_low[...], w()).astype(BF16)

    def self_back(h):
        hs = head_of(h)
        for g in range(groups):
            at = group_of(g)
            probs = self_probs(g, hs)
            given = mix_grad[at, hs]
            queries, keyed, valued = self_q[at, hs], self_k[at, hs], self_v[at, hs]
            prob_grad = dot_nt(given, valued)
            inner = jnp.sum(self_mix[at, hs].astype(F32) * given.astype(F32), axis=-1, keepdims=True)
            logit_grad = (probs * (prob_grad - inner)).astype(BF16)
            self_q[at, hs] = (dot_nn(logit_grad, keyed) * SCALE).astype(BF16)
            self_k[at, hs] = (dot_tn(logit_grad, queries) * SCALE).astype(BF16)
            self_v[at, hs] = dot_tn(probs.astype(BF16), given).astype(BF16)

    each(HEADS // 2, self_back, 2)
    turn(False)
    each(HEADS // 2, lambda i: self_back(HEADS // 2 + i), 2)
    turn()
    w = weights.use(S_Q)
    part[...] = dot_nt(self_q[...], w())
    w = weights.use(S_K)
    part[...] += dot_nt(self_k[...], w())
    w = weights.use(S_V)
    part[...] += dot_nt(self_v[...], w())
    turn()

    def back_one(i):
        at = span_of(i)
        pull, gain_part, _ = norm_back(res_one[at, :], gain_of(2), part[at, :])
        total = grad[at, :] + pull
        grad[at, :] = total
        res_low[at, :] = total.astype(BF16)
        gain_add(2, gain_part)

    each(rows // tile, back_one, 2)
    turn()

    def sum_groups(i):
        total = grad[span_of(i), :]
        for g in range(1, groups):
            total += grad[pl.ds(pl.multiple_of(g * LAT + i * tile, tile), tile), :]
        lat_grad[span_of(i), :] = total

    each(LAT // tile, sum_groups)
    w = weights.use(W_O)
    mix_grad[...] = dot_nt(res_low[...], w()).astype(BF16)
    turn()

    def cross_back(h):
        hs = head_of(h)
        logits = dot_nt(query[:, hs], keys[:, hs]) * (SCALE * LOG2_E)
        here = lax.broadcasted_iota(jnp.int32, (LAT, HEAD), 1) == h
        made = None
        for g in range(groups):
            at = group_of(g)
            given = mix_grad[at, hs]
            prob_grad = dot_nt(given, values[:, hs])
            total = jnp.sum(jnp.where(here, lse[at, :], 0.0), axis=-1, keepdims=True)
            inner = jnp.sum(cross_mix[at, hs].astype(F32) * given.astype(F32), axis=-1, keepdims=True)
            probs = jnp.exp2(logits + count_log[pl.ds(g, 1), :] - total)
            low = probs.astype(BF16)
            wide[at, :] = low[:, :half]
            wide[pl.ds(rows + g * LAT, LAT), :] = low[:, half:]
            pulled = probs * (prob_grad - inner)
            made = pulled if g == 0 else made + pulled
        logit_grad = made.astype(BF16)
        asked = query[:, hs]
        query_back = dot_nn(logit_grad, keys[:, hs]) * SCALE
        keys[:, hs] = (dot_tn(logit_grad, asked) * SCALE).astype(BF16)
        query[:, hs] = query_back.astype(BF16)
        for side in range(2):
            probs = wide[pl.ds(side * rows, rows), :]
            values[pl.ds(side * half, half), hs] = dot_tn(probs, mix_grad[:, hs]).astype(BF16)

    point_load.start()
    for part_at in range(4):
        each(2, lambda i, part_at=part_at: cross_back(part_at * 2 + i))
        turn(False)

    w = weights.use(W_Q)
    pull, gain_part, _ = norm_back(lat[...], gain_of(0), dot_nt(query[...], w()))
    lat_grad[...] += pull
    gain_add(0, gain_part)

    point_load.wait()
    each(slots // tile, norm_points, 4)
    turn()
    w_keys, w_values = weights.use(W_K), weights.use(W_V, keep=1)
    point_stores = []
    for block in range(slots // 512):
        at = pl.ds(block * 512, 512)
        part[...] = dot_nt(keys[at, :], w_keys()) + dot_nt(values[at, :], w_values())

        def back_points(i, block=block):
            row = pl.ds(pl.multiple_of(block * 512 + i * tile, tile), tile)
            pull, gain_part, _ = norm_back(slope[row, :].astype(F32), gain_of(1), part[span_of(i), :])
            slope[row, :] = pull.astype(BF16)
            gain_add(1, gain_part)

        each(512 // tile, back_points, 2)
        store = pltpu.make_async_copy(slope.at[at], r["point_grad"].at[at], r["point_sem"].at[block])
        store.start()
        point_stores.append(store)
        turn(block < 2)
    while len(getattr(reduce, "begun", ())) < len(QUEUE) and linked or not linked and reduce.count < len(QUEUE):
        turn()
    reduce.finish()
    for store in point_stores:
        store.wait()


def layer_call(linked, small, attn, up, down, points, near, lens, cot):
    slots, rows, groups = points.shape[0], cot.shape[0], near.shape[0]
    any_space = pl.BlockSpec(memory_space=pl.ANY)
    in_vmem = pl.BlockSpec(memory_space=pltpu.VMEM)
    in_smem = pl.BlockSpec(memory_space=pltpu.SMEM)
    shape = jax.ShapeDtypeStruct
    split = (2,) * 5
    outs = [shape((rows, D), BF16), shape((slots, D), BF16)]
    out_specs = [any_space, any_space]
    if linked:
        outs += [shape((PART, SMALL), F32)] + [shape((PART, D), F32)] * 8
        outs += [shape((PART, FF), F32), shape((QUARTERS * PART, D), F32)]
        out_specs += [any_space] * 11
        outs += [shape((CHUNKS, *split, PART, D), BF16), shape((*split, PART, SMALL), BF16)]
        out_specs += [any_space] * 2
    else:
        outs += [shape((D, SMALL), F32)] + [shape((D, D), BF16)] * 8
        outs += [shape((QUARTERS, D, D), BF16), shape((FF, D), BF16)]
        out_specs += [in_vmem] + [any_space] * 10
    vmem, dma = pltpu.VMEM, pltpu.SemaphoreType.DMA
    scratch = {
        "keys": vmem((slots, D), BF16),
        "values": vmem((slots, D), BF16),
        "wide": vmem((QUARTERS * rows, D), BF16),
        "slope": vmem((QUARTERS * rows, D), BF16),
    }
    for name in ("cross_mix", "self_mix", "h_s", "h_m", "self_q", "self_k", "self_v", "res_low", "mix_grad"):
        scratch[name] = vmem((rows, D), BF16)
    for name in ("res_one", "res_two", "grad", "part"):
        scratch[name] = vmem((rows, D), F32)
    scratch |= {
        "lat": vmem((LAT, D), F32),
        "h_q": vmem((LAT, D), BF16),
        "query": vmem((LAT, D), BF16),
        "lse": vmem((rows, HEAD), F32),
        "gains": vmem((8, D), F32),
        "gain_grads": vmem((8, D), F32),
        "count_log": vmem((groups, slots), F32),
        "held": vmem((WEIGHT_SLOTS, *split, PART, D), BF16),
        "held_sem": dma((WEIGHT_SLOTS,)),
        "point_sem": dma((slots // 512,)),
        "tiny_sem": dma((2,)),
    }
    if linked:
        scratch["term"] = vmem((TERM_SLOTS, 2, 2, 2, 2, 2, PART, D), BF16)
        for stage in range(STAGES):
            scratch[f"land{stage}"] = vmem((LAND_SLOTS, *(2,) * (4 - stage), PART, D), BF16)
        pieces = 2 * CHUNKS + 1
        scratch |= {
            "g_send": dma((pieces, STAGES)),
            "g_recv": dma((pieces, STAGES)),
            "own_sem": dma((CHUNKS + 1,)),
            "r_send": dma((len(QUEUE), STAGES, 3)),
            "r_recv": dma((len(QUEUE), STAGES, 3)),
            "credit": pltpu.SemaphoreType.REGULAR((STAGES, 3, 5)),
            "final_sem": dma((2 + QUARTERS,)),
        }
    else:
        scratch |= {"term": vmem((2, 512, D), BF16), "term_sem": dma((2,))}
    names = NAMES_IN + NAMES_OUT + (("full", "full_small") if linked else ()) + tuple(scratch)
    params = {"collective_id": 0} if linked else {}
    return pl.pallas_call(
        functools.partial(layer_kernel, linked, names),
        out_shape=outs,
        in_specs=[in_vmem if linked else any_space] + [any_space] * 8 + [in_vmem if linked else any_space] + [any_space] * 2 + [in_vmem, in_smem, in_vmem],
        out_specs=out_specs,
        scratch_shapes=list(scratch.values()),
        compiler_params=pltpu.CompilerParams(has_side_effects=True, vmem_limit_bytes=63 << 20, **params),
    )(small, *attn, up, down, points, near, lens, cot)


HAND_ROWS = 512


def hand_over_kernel(count, small, *refs):
    sources, (lat_out, *targets) = refs[:count], refs[count : 2 * count + 1]
    gains = refs[2 * count + 1 : 2 * count + 5]
    stages, load_sem, store_sem = refs[2 * count + 5 : -2], refs[-2], refs[-1]
    loads, stores = [], []
    for source, target, stage in zip(sources, targets, stages, strict=True):
        for row in range(0, source.shape[0], HAND_ROWS):
            at, i = pl.ds(row, min(HAND_ROWS, source.shape[0])), len(loads)
            loads.append(pltpu.make_async_copy(source.at[at], stage.at[at], load_sem.at[i]))
            stores.append(pltpu.make_async_copy(stage.at[at], target.at[at], store_sem.at[i]))
    for load in loads:
        load.start()
    lat_out[...] = small[:, pl.ds(0, LAT)]
    turned = small[...].T
    for i, gain in enumerate(gains):
        gain[...] = turned[LAT + i : LAT + i + 1]
    for load, store in zip(loads, stores, strict=True):
        load.wait()
        store.start()
    for store in stores:
        store.wait()


def hand_over(made):
    out, point_grad, small, *grads = made
    moved = [point_grad, out, *grads]
    any_space = pl.BlockSpec(memory_space=pl.ANY)
    in_vmem = pl.BlockSpec(memory_space=pltpu.VMEM)
    own = small.shape[0]
    count = sum(max(one.shape[0] // HAND_ROWS, 1) for one in moved)
    lat_out, point_grad, out, *rest = pl.pallas_call(
        functools.partial(hand_over_kernel, len(moved)),
        out_shape=[jax.ShapeDtypeStruct((own, LAT), F32)]
        + [jax.ShapeDtypeStruct(one.shape, one.dtype) for one in moved]
        + [jax.ShapeDtypeStruct((1, own), F32)] * 4,
        in_specs=[in_vmem] + [any_space] * len(moved),
        out_specs=[in_vmem] + [any_space] * len(moved) + [in_vmem] * 4,
        scratch_shapes=[pltpu.VMEM(one.shape, one.dtype) for one in moved]
        + [pltpu.SemaphoreType.DMA((count,))] * 2,
        compiler_params=pltpu.CompilerParams(vmem_limit_bytes=60 << 20),
    )(small, *moved)
    return (out, point_grad, lat_out, *rest)


def on_device(
    linked, latents, gain_q, gain_kv, w_q, w_k, w_v, w_o, gain_s, s_q, s_k, s_v, s_o, gain_m, w_up, w_down,
    points, neighbours, lengths, cotangent,
):
    split = (2,) * 5
    lane = lax.broadcasted_iota(jnp.int32, (1, SMALL), 1)
    small = jnp.pad(latents.T, ((0, 0), (0, SMALL - LAT)))
    for i, gain in enumerate((gain_q, gain_kv, gain_s, gain_m)):
        small = jnp.where(lane == LAT + i, gain[:, None], small)
    attn = (w_k, w_v, w_q, w_o, s_q, s_k, s_v, s_o)
    if linked:
        made = layer_call(True, small, attn, w_up, w_down, points, neighbours, lengths, cotangent)[: len(NAMES_OUT)]
        out, point_grad, turned, g_k, g_v, g_q, g_o, gs_q, gs_k, gs_v, gs_o, g_up, g_down, *gains = hand_over(made)
        turned = turned.T
        gains = [gain.reshape(-1) for gain in gains]
    else:
        gathered = lambda shard: lax.all_gather(shard, AXES, axis=0, tiled=True)
        blocks = lambda whole: whole.reshape(*split, PART, whole.shape[-1])
        up = gathered(w_up).reshape(D, QUARTERS, D).transpose(1, 0, 2).reshape(QUARTERS, *split, PART, D)
        down = gathered(w_down).reshape(QUARTERS, *split, PART, D)
        made = layer_call(
            False, blocks(gathered(small)), [blocks(gathered(one)) for one in attn], up, down,
            points, neighbours, lengths, cotangent,
        )
        out, point_grad = made[:2]
        summed = lambda whole: lax.psum_scatter(whole.astype(F32), AXES, scatter_dimension=0, tiled=True)
        g_small, g_k, g_v, g_q, g_o, gs_q, gs_k, gs_v, gs_o = [summed(one) for one in made[2:11]]
        g_up = summed(made[11].transpose(1, 0, 2).reshape(D, FF))
        g_down = summed(made[12])
        turned = g_small.T[:LAT]
        gains = [g_small[:, LAT + i] for i in range(4)]
    return (
        out, point_grad, turned, gains[0], gains[1], g_q, g_k, g_v, g_o,
        gains[2], gs_q, gs_k, gs_v, gs_o, gains[3], g_up, g_down,
    )


def solution(mesh):
    linked = (mesh.shape["dp"], mesh.shape["fsdp"]) == LINKED_MESH
    row, vector, matrix = P(None, AXES), P(AXES), P(AXES, None)
    return jax.shard_map(
        functools.partial(on_device, linked),
        mesh=mesh,
        in_specs=(
            row, vector, vector, matrix, matrix, matrix, matrix, vector, matrix, matrix, matrix, matrix, vector,
            matrix, matrix, matrix, matrix, vector, matrix,
        ),
        out_specs=(
            matrix, matrix, row, vector, vector, matrix, matrix, matrix, matrix,
            vector, matrix, matrix, matrix, matrix, vector, matrix, matrix,
        ),
        check_vma=False,
    )
```
